128 devices in a mesh: cluster: 8 (over z, core), member: 16 (over y, x).
Axes of the slice: x: 4, y: 4, z: 4, core: 2. Of those that a mesh axis runs over, the one named last changes fastest.
Arguments:
- cam_jac: bfloat16 [18, 8, 65536], P(None, None, ('cluster', 'member')), may hold values from -0.3125 to 0.3125
- point_jac: bfloat16 [6, 8, 65536], P(None, None, ('cluster', 'member')), may hold values from -6 to 6
- residuals: bfloat16 [2, 8, 65536], P(None, None, ('cluster', 'member')), may hold values from -6 to 6
- obs_camera: int32 [8, 65536], P(None, ('cluster', 'member')), may hold values from 0 to 2047, as said below
- obs_count: int32 [65536], P(('cluster', 'member')), may hold values from 2 to 8, as said below
- new_cluster: int32 [2048], replicated, may hold values from 0 to 7, as said below
- new_slot: int32 [2048], replicated, may hold values from 0 to 255, as said below
Outputs:
- reduced_system: float32 [18432, 2304], P(('cluster', 'member'))
- camera_step: float32 [18432], P(('cluster', 'member'))
The draws below stay inside these ranges and needn't reach their ends.
Inputs may be any that keep to these rules, and one draw needn't show every extreme that they name: `obs_camera`: old ids: camera i lies in old cluster i // 256; a point block stored on the devices of cluster c observes cameras of old cluster c only, distinct ones in all its slots. Its live observations lie in new cluster c except at most two that lie in a single other new cluster. On every device, for each other cluster, at most 16 point blocks have live observations there, and exactly 16 for some other cluster. `obs_count`: some point block of every device has 8 live observations. `new_cluster`: each old cluster keeps all but 64 of its cameras; every new cluster holds exactly 256 cameras. `new_slot`: cameras of one new cluster have distinct rows.
All inputs are finite; a program needn't handle non-finite values.
Results may differ from the reference program's by a relative error of at most 0.0038.
Values may be sent and summed in bfloat16 or wider, within the bound.
No kernel may reach another device: no remote copies, remote signals or barrier semaphores. Data moves between devices by JAX's collectives and lax.ppermute only.
A program may use at most 192 MiB of HBM per device.

```python
import jax
import jax.numpy as jnp
from jax import lax

SHOTS_EACH_BATCH = 256
PANEL = 16
OBS = 8
MOVE = 64
BCAP = 16
PT_DEV = 512
POINTS = 65536
N_CLUSTER = 8
N_MEMBER = 16


def viewpoint_arrangement(key):
    cluster_count = N_CLUSTER
    first_keys = jax.random.split(jax.random.fold_in(key, 101), cluster_count)
    tiebreak_keys = jax.random.split(jax.random.fold_in(key, 102), cluster_count)
    mixed_slot_number = jax.vmap(lambda iteration_tally: jax.random.permutation(iteration_tally, SHOTS_EACH_BATCH))(first_keys).astype(jnp.int32)
    relabel_batch_items = jax.vmap(lambda iteration_tally: jax.random.permutation(iteration_tally, SHOTS_EACH_BATCH))(tiebreak_keys).astype(jnp.int32)
    clusters = jnp.arange(cluster_count, dtype=jnp.int32)[:, None]
    moving = mixed_slot_number < MOVE
    aimed_batch = jnp.where(moving, (clusters + 1 + mixed_slot_number % (cluster_count - 1)) % cluster_count, clusters)
    renamed_measurements = relabel_batch_items[aimed_batch, mixed_slot_number]
    landmark_inverse_tiles = jnp.argsort(mixed_slot_number, axis=1).astype(jnp.int32)
    return (aimed_batch.astype(jnp.int32), renamed_measurements.astype(jnp.int32), landmark_inverse_tiles)


def observation_layout(key):
    cluster_count = N_CLUSTER
    device_count = N_CLUSTER * N_MEMBER
    aimed_batch, renamed_measurements, landmark_inverse_tiles = viewpoint_arrangement(key)
    point_key = jax.random.fold_in(key, 103)
    device_ids = jnp.arange(device_count, dtype=jnp.int32)

    def one_device(device):
        device_key = jax.random.fold_in(point_key, device)
        home_cluster = device // N_MEMBER
        device_keys = jax.random.split(device_key, 7)
        group_loads = jax.random.randint(device_keys[0], (cluster_count - 1,), max(1, BCAP // 4), BCAP + 1)
        fullest = jax.random.randint(device_keys[1], (), 0, cluster_count - 1)
        group_loads = jnp.where(jnp.arange(cluster_count - 1) == fullest, BCAP, group_loads)
        padded_loads = jnp.concatenate([group_loads, jnp.zeros((1,), jnp.int32)])
        shuffled = jax.random.permutation(device_keys[2], PT_DEV).astype(jnp.int32)
        group_index = jnp.minimum(shuffled // BCAP, cluster_count - 1)
        within = shuffled % BCAP
        boundary = (group_index < cluster_count - 1) & (within < padded_loads[group_index])
        counts = jax.random.randint(device_keys[3], (PT_DEV,), 2, OBS + 1)
        counts = counts.at[0].set(OBS)
        movers = jnp.where(counts >= 3, jax.random.randint(device_keys[4], (PT_DEV,), 1, 3), 1)
        remaining_labels = jax.random.split(device_keys[5], PT_DEV)
        stayers = jax.vmap(lambda iteration_tally: jax.random.permutation(iteration_tally, SHOTS_EACH_BATCH - MOVE)[:OBS])(remaining_labels).astype(jnp.int32) + MOVE
        per_group = jnp.maximum((MOVE - group_index + cluster_count - 2) // (cluster_count - 1), 2)
        random_ints = jax.random.randint(device_keys[6], (PT_DEV, 4), 0, 1 << 20)
        first_pick = random_ints[:, 0] % per_group
        second_pick = (first_pick + 1 + random_ints[:, 1] % (per_group - 1)) % per_group
        first_spot = random_ints[:, 2] % counts
        second_spot = (first_spot + 1 + random_ints[:, 3] % (counts - 1)) % counts
        first_rank = group_index + (cluster_count - 1) * first_pick
        second_rank = group_index + (cluster_count - 1) * second_pick
        slot_index = jnp.arange(OBS, dtype=jnp.int32)[None, :]
        use_first = boundary[:, None] & (slot_index == first_spot[:, None])
        use_second = boundary[:, None] & (movers[:, None] == 2) & (slot_index == second_spot[:, None])
        chosen = jnp.where(use_first, first_rank[:, None], jnp.where(use_second, second_rank[:, None], stayers))
        local_ids = landmark_inverse_tiles[home_cluster][chosen]
        return ((home_cluster * SHOTS_EACH_BATCH + local_ids).T.astype(jnp.int32), counts.astype(jnp.int32))
    cameras, counts = jax.vmap(one_device)(device_ids)
    return (cameras.transpose(1, 0, 2).reshape(OBS, device_count * PT_DEV), counts.reshape(-1))


def draw_obs_camera(key, part):
    return observation_layout(key)[0]


def draw_obs_count(key, part):
    return observation_layout(key)[1]


def draw_new_cluster(key, part):
    return viewpoint_arrangement(key)[0].reshape(-1)


def draw_new_slot(key, part):
    return viewpoint_arrangement(key)[1].reshape(-1)


def block_levels(stream_key, shape, shards, smallest, top_value):
    loudness = 1.0
    for dim, shards_of in shards:
        heights = jax.random.uniform(jax.random.fold_in(jax.random.fold_in(stream_key, 6), dim), (shards_of,), jnp.float32, smallest / len(shards), top_value / len(shards))
        loudness = loudness * jnp.repeat(jnp.exp(heights), shape[dim] // shards_of).reshape((-1,) + (1,) * (len(shape) - 1 - dim))
    return loudness


def normal_values(rng, dims, spread, reach, cuts=(), held_as=jnp.bfloat16):
    values = jax.random.normal(rng, dims, jnp.float32) * spread
    if len(cuts) > 0:
        values = block_levels(rng, dims, cuts, -0.22, 0.18) * values
    return jnp.clip(values, min=-reach, max=reach).astype(held_as)


def setup_inputs(seed: int = 0) -> dict:
    splits = jax.random.split(jax.random.key(seed), 8)
    return {
        "cam_jac": normal_values(splits[0], (18, OBS, POINTS), (10 * PT_DEV * N_MEMBER // SHOTS_EACH_BATCH) ** -0.5, 0.3125, ((2, 128),)),
        "point_jac": normal_values(splits[1], (6, OBS, POINTS), 1.0, 6.0, ((2, 128),)),
        "residuals": normal_values(splits[2], (2, OBS, POINTS), 1.0, 6.0, ((2, 128),)),
        "obs_camera": draw_obs_camera(jax.random.fold_in(splits[7], 71), 0),
        "obs_count": draw_obs_count(jax.random.fold_in(splits[7], 71), 0),
        "new_cluster": draw_new_cluster(jax.random.fold_in(splits[7], 71), 0),
        "new_slot": draw_new_slot(jax.random.fold_in(splits[7], 71), 0),
    }


DAMPING = 0.5
EXACT_PRECISION = lax.Precision.HIGHEST

def invert_three(matrix):

    def cofactor(i, j):
        keep_rows = [r for r in range(3) if r != i]
        keep_cols = [r for r in range(3) if r != j]
        minor_value = matrix[keep_rows[0], keep_cols[0]] * matrix[keep_rows[1], keep_cols[1]] - matrix[keep_rows[0], keep_cols[1]] * matrix[keep_rows[1], keep_cols[0]]
        sign_value = 1.0 if (i + j) % 2 == 0 else -1.0
        return sign_value * minor_value
    cofactors = [[cofactor(i, j) for j in range(3)] for i in range(3)]
    determinant = matrix[0, 0] * cofactors[0][0] + matrix[0, 1] * cofactors[0][1] + matrix[0, 2] * cofactors[0][2]
    adjugate = jnp.stack([jnp.stack([cofactors[j][i] for j in range(3)]) for i in range(3)])
    return adjugate / determinant

def eliminate(cam_part, point_part, resid_part, slot_rows):
    valid_mask = (slot_rows >= 0).astype(jnp.float32)
    obs_slots = slot_rows.shape[0]
    block_count = slot_rows.shape[1]
    camera_rows = (cam_part.astype(jnp.float32) * valid_mask).reshape(2, 9, obs_slots, block_count)
    point_rows = (point_part.astype(jnp.float32) * valid_mask).reshape(2, 3, obs_slots, block_count)
    resid_rows = resid_part.astype(jnp.float32) * valid_mask
    normal_point = jnp.einsum('kbon,kcon->bcn', point_rows, point_rows, precision=EXACT_PRECISION) + DAMPING * jnp.eye(3, dtype=jnp.float32)[:, :, None]
    point_grad = jnp.einsum('kbon,kon->bn', point_rows, resid_rows, precision=EXACT_PRECISION)
    landmark_inverse_tiles = invert_three(normal_point)
    camera_point_coupling = jnp.einsum('kaon,kbon->abon', camera_rows, point_rows, precision=EXACT_PRECISION).astype(jnp.bfloat16)
    reduced_camera_matrix = jnp.einsum('wrsd,rpd->wpsd', camera_point_coupling.astype(jnp.float32), landmark_inverse_tiles, precision=EXACT_PRECISION).astype(jnp.bfloat16)
    camera_normal = jnp.einsum('kaon,kcon->acon', camera_rows, camera_rows, precision=EXACT_PRECISION)
    camera_grad = jnp.einsum('kaon,kon->aon', camera_rows, resid_rows, precision=EXACT_PRECISION) - jnp.einsum('abon,bn->aon', reduced_camera_matrix.astype(jnp.float32), point_grad, precision=EXACT_PRECISION)
    camera_terms = jnp.concatenate([camera_normal.reshape(81, obs_slots, block_count), camera_grad], axis=0)
    return (camera_point_coupling, reduced_camera_matrix, camera_terms)

def reference(cam_jac, point_jac, residuals, obs_camera, obs_count, new_cluster, new_slot):
    total_points = obs_camera.shape[1]
    block_total = total_points // PT_DEV
    live_mask = lax.broadcasted_iota(jnp.int32, obs_camera.shape, 0) < obs_count[None, :]
    cluster_of = jnp.take(new_cluster, obs_camera)
    row_of = jnp.take(new_slot, obs_camera)

    def blocked(array):
        shaped = array.reshape(array.shape[:-1] + (block_total, PT_DEV))
        return jnp.moveaxis(shaped, -2, 0)
    cam_blocks = blocked(cam_jac)
    point_blocks = blocked(point_jac)
    resid_blocks = blocked(residuals)
    panel_width = 9 * PANEL
    panel_total = SHOTS_EACH_BATCH // PANEL
    system_list = []
    solved_step_list = []
    for cluster in range(N_CLUSTER):
        slot_rows = jnp.where(live_mask & (cluster_of == cluster), row_of, -1).astype(jnp.int32)
        slot_blocks = blocked(slot_rows)

        def accumulate(carry_pair, block_items):
            flat_sum, camera_total = carry_pair
            cam_part, point_part, resid_part, slot_part = block_items
            camera_point_coupling, reduced_camera_matrix, camera_terms = eliminate(cam_part, point_part, resid_part, slot_part)
            pair_blocks = jnp.einsum('abjn,cbkn->njkac', reduced_camera_matrix.astype(jnp.float32), camera_point_coupling.astype(jnp.float32), precision=EXACT_PRECISION)
            safe_ids = jnp.where(slot_part < 0, SHOTS_EACH_BATCH, slot_part).astype(jnp.int32)
            id_rows = safe_ids.T
            flat_index = (id_rows[:, :, None] * (SHOTS_EACH_BATCH + 1) + id_rows[:, None, :]).reshape(-1)
            flat_sum = flat_sum.at[flat_index].add(pair_blocks.reshape(-1, 9, 9))
            per_camera = jax.ops.segment_sum(camera_terms.reshape(90, -1).T, safe_ids.reshape(-1), num_segments=SHOTS_EACH_BATCH + 1)
            camera_total = camera_total + per_camera[:SHOTS_EACH_BATCH].T
            return ((flat_sum, camera_total), None)
        start_state = (jnp.zeros(((SHOTS_EACH_BATCH + 1) * (SHOTS_EACH_BATCH + 1), 9, 9), jnp.float32), jnp.zeros((90, SHOTS_EACH_BATCH), jnp.float32))
        (flat_sum, camera_total), _ = lax.scan(accumulate, start_state, (cam_blocks, point_blocks, resid_blocks, slot_blocks))
        pair_total = flat_sum.reshape(SHOTS_EACH_BATCH + 1, SHOTS_EACH_BATCH + 1, 9, 9)[:SHOTS_EACH_BATCH, :SHOTS_EACH_BATCH].transpose(0, 2, 1, 3).reshape(9 * SHOTS_EACH_BATCH, 9 * SHOTS_EACH_BATCH)
        normal_blocks = camera_total[:81].reshape(9, 9, SHOTS_EACH_BATCH) + DAMPING * jnp.eye(9, dtype=jnp.float32)[:, :, None]
        identity_cams = jnp.eye(SHOTS_EACH_BATCH, dtype=jnp.float32)
        block_diag = (normal_blocks.transpose(2, 0, 1)[:, :, None, :] * identity_cams[:, None, :, None]).reshape(9 * SHOTS_EACH_BATCH, 9 * SHOTS_EACH_BATCH)
        reduced_matrix = block_diag - pair_total
        gradient = camera_total[81:].T.reshape(-1)
        diagonal = jnp.stack([reduced_matrix[q * panel_width:(q + 1) * panel_width, q * panel_width:(q + 1) * panel_width] for q in range(panel_total)])
        factor = jnp.linalg.cholesky(diagonal)
        solved = jax.scipy.linalg.cho_solve((factor, True), gradient.reshape(panel_total, panel_width)[..., None])[..., 0]
        system_list.append(reduced_matrix)
        solved_step_list.append(-solved.reshape(-1))
    return (jnp.concatenate(system_list, axis=0), jnp.concatenate(solved_step_list, axis=0))
```

```python
import jax
import jax.numpy as jnp
from jax import lax
from jax.experimental import pallas as pl
from jax.experimental.pallas import tpu as pltpu
from jax.sharding import PartitionSpec as P

CAMS = 256
OWN = 16
OBS = 8
PTS = 512
FAR = 128
ALL = PTS + FAR
CAP = 256
ROWS = 224
SLOT = 208
COUNT = 216
OVER = 217
ROUNDS = -(-ALL // CAP)
DAMPING = 0.5
EXACT = lax.Precision.HIGHEST
F32 = jnp.float32
BF16 = jnp.bfloat16
NT = (((1,), (1,)), ((), ()))
VMEM_BYTES = 56 * 1024 * 1024


def iota(shape, dim):
    return lax.broadcasted_iota(jnp.int32, shape, dim)


def running_count(hits):
    tri = (iota((128, 128), 0) <= iota((128, 128), 1)).astype(BF16)
    parts = []
    base = jnp.zeros((hits.shape[0], 1), F32)
    for t in range(hits.shape[1] // 128):
        part = hits[:, t * 128 : (t + 1) * 128]
        parts.append(jnp.dot(part.astype(BF16), tri, preferred_element_type=F32) + base)
        base = base + jnp.sum(part, axis=1, keepdims=True)
    return jnp.concatenate(parts, axis=1)


def sort_out_kernel(cam_ref, pt_ref, res_ref, oc_ref, cnt_ref, ncl_ref, nsl_ref, slot_ref, far_ref):
    ids = oc_ref[...]
    cluster = ids >> 8
    old = cluster[0:1, 0:128]
    code = ncl_ref[...] * CAMS + nsl_ref[...]
    row = iota((16, 128), 0)
    tables = [
        jnp.sum(jnp.where(row == 2 * old + t, code, 0), axis=0, keepdims=True) for t in range(2)
    ]
    tables = [jnp.broadcast_to(t, (OBS, 128)) for t in tables]
    found = []
    for t in range(PTS // 128):
        local = ids[:, t * 128 : (t + 1) * 128] & 255
        lane = local & 127
        low, high = [
            jnp.take_along_axis(table, lane, axis=1, mode="promise_in_bounds") for table in tables
        ]
        found.append(jnp.where(local < 128, low, high))
    found = jnp.concatenate(found, axis=1)
    aim = found >> 8
    place = (found & 255) + 1
    live = iota((OBS, PTS), 0) < cnt_ref[...]
    home = jnp.where(live & (aim == cluster), place, 0)
    abroad = live & (aim != cluster)
    away = jnp.where(abroad, place, 0)
    slot_ref[0:8, :] = home.astype(F32).astype(BF16)
    slot_ref[8:16, :] = jnp.zeros((8, PTS), BF16)
    target = jnp.max(jnp.where(abroad, aim, -1), axis=0, keepdims=True)
    hits = (jnp.broadcast_to(target, (8, PTS)) == iota((8, PTS), 0)).astype(F32)
    rank = jnp.sum((running_count(hits) - 1.0) * hits, axis=0, keepdims=True)
    column = jnp.where(target >= 0, target * 16 + rank.astype(jnp.int32), -1)
    chooser = (jnp.broadcast_to(column, (FAR, PTS)) == iota((FAR, PTS), 0)).astype(BF16)
    mask = abroad.astype(F32)
    mask2 = jnp.concatenate([mask, mask], axis=0).astype(BF16)

    def send(ref, groups):
        rows = jnp.concatenate([ref[16 * g : 16 * g + 16, :] * mask2 for g in range(groups)], axis=0)
        return lax.dot_general(chooser, rows, NT, preferred_element_type=F32)

    far_ref[:, 0:208] = jnp.concatenate(
        [send(cam_ref, 9), send(pt_ref, 3), send(res_ref, 1)], axis=1
    ).astype(BF16)
    slots = jnp.concatenate([away.astype(F32), jnp.zeros((40, PTS), F32)], axis=0).astype(BF16)
    far_ref[:, 208:256] = lax.dot_general(
        chooser, slots, NT, preferred_element_type=F32
    ).astype(BF16)


def pack_kernel(first_rank, cam_ref, pt_ref, res_ref, slot_ref, far_ref, out_ref, feat):
    feat[0:144, 0:PTS] = cam_ref[...]
    feat[144:192, 0:PTS] = pt_ref[...]
    feat[192:208, 0:PTS] = res_ref[...]
    feat[208:224, 0:PTS] = slot_ref[...]
    feat[:, PTS:ALL] = far_ref[...].astype(F32).T[0:ROWS, :].astype(BF16)
    slots = feat[208:224, :].astype(F32)[0:8, :].astype(jnp.int32)
    owner = ((slots + 15) >> 4) - 1
    member = iota((16, ALL), 0)
    touch = jnp.zeros((16, ALL), jnp.bool_)
    for o in range(OBS):
        touch = touch | (jnp.broadcast_to(owner[o : o + 1, :], (16, ALL)) == member)
    hits = touch.astype(F32)
    count = running_count(hits)
    total = jnp.max(count, axis=1, keepdims=True)
    rank = count - 1.0 - first_rank
    rank = jnp.where(touch & (rank >= 0.0) & (rank < CAP), rank, -1.0)
    over = jnp.max((total > CAP).astype(F32), axis=0, keepdims=True)
    seat = iota((CAP, ALL), 0).astype(F32)
    here = jnp.clip(total - first_rank, 0.0, float(CAP))
    line = iota((16, CAP), 0)
    for d in range(16):
        chosen = (jnp.broadcast_to(rank[d : d + 1, :], (CAP, ALL)) == seat).astype(BF16)
        moved = lax.dot_general(feat[...], chosen, NT, preferred_element_type=F32)
        out_ref[d, 0:208, :] = moved[0:208, :].astype(BF16)
        tail = jnp.where(
            line < 8,
            moved[208:224, :],
            jnp.where(line == 8, here[d : d + 1, :], jnp.where(line == 9, over, 0.0)),
        )
        out_ref[d, 208:224, :] = tail.astype(BF16)


def block_values(f):
    slot = f[SLOT : SLOT + 8, :]
    valid = slot > 0.0
    cam = [[f[(k * 9 + a) * 8 : (k * 9 + a) * 8 + 8, :] for a in range(9)] for k in range(2)]
    pt = [
        [
            jnp.where(valid, f[144 + (k * 3 + b) * 8 : 152 + (k * 3 + b) * 8, :], 0.0)
            for b in range(3)
        ]
        for k in range(2)
    ]
    res = [jnp.where(valid, f[192 + k * 8 : 200 + k * 8, :], 0.0) for k in range(2)]

    def over_obs(x):
        return jnp.sum(x, axis=0, keepdims=True)

    v = {}
    for b in range(3):
        for c in range(b, 3):
            v[b, c] = over_obs(pt[0][b] * pt[0][c] + pt[1][b] * pt[1][c]) + (
                DAMPING if b == c else 0.0
            )
            v[c, b] = v[b, c]
    g = [over_obs(pt[0][b] * res[0] + pt[1][b] * res[1]) for b in range(3)]

    def cofactor(i, j):
        r = [x for x in range(3) if x != i]
        c = [x for x in range(3) if x != j]
        minor = v[r[0], c[0]] * v[r[1], c[1]] - v[r[0], c[1]] * v[r[1], c[0]]
        return minor if (i + j) % 2 == 0 else -minor

    cof = {(i, j): cofactor(i, j) for i in range(3) for j in range(i, 3)}
    det = v[0, 0] * cof[0, 0] + v[0, 1] * cof[0, 1] + v[0, 2] * cof[0, 2]
    inv = {}
    for i in range(3):
        for j in range(i, 3):
            inv[i, j] = cof[i, j] / det
            inv[j, i] = inv[i, j]
    w = {}
    z = {}
    for a in range(9):
        for b in range(3):
            w[a, b] = (cam[0][a] * pt[0][b] + cam[1][a] * pt[1][b]).astype(BF16).astype(F32)
        for b in range(3):
            z[a, b] = w[a, 0] * inv[0, b] + w[a, 1] * inv[1, b] + w[a, 2] * inv[2, b]
    return slot, cam, res, w, z, g


def system_kernel(
    blocks, m_ref, x_ref, out_ref, step_ref, wv, wp, zp, ap, gp, acc, acc_u, acc_g, turned, dm, st, woven
):
    m = m_ref[0]
    acc[...] = jnp.zeros_like(acc)
    acc_u[...] = jnp.zeros_like(acc_u)
    acc_g[...] = jnp.zeros_like(acc_g)
    gp[...] = jnp.zeros_like(gp)
    names = (iota((16, 128), 0) + 1).astype(F32).astype(BF16)

    def spread(row):
        return jnp.broadcast_to(row, (16, 128)).astype(BF16)

    def choose(slots, own, values):
        out = jnp.zeros((16, 128), BF16)
        for o in range(OBS):
            out = jnp.where(slots[o] == own, values[o], out)
        return out

    def chunk(s, carry):
        slot, cam, res, w, z, g = block_values(x_ref[s].astype(F32))
        for a in range(9):
            for b in range(3):
                wv[(a * 3 + b) * 8 : (a * 3 + b) * 8 + 8, :] = w[a, b]
        for b in range(3):
            high = g[b].astype(BF16)
            rest = g[b] - high.astype(F32)
            mid = rest.astype(BF16)
            low = (rest - mid.astype(F32)).astype(BF16)
            rows = jnp.concatenate(
                [high.astype(F32), mid.astype(F32), low.astype(F32), jnp.zeros((13, CAP), F32)], axis=0
            )
            gp[:, b * CAP : (b + 1) * CAP] = rows.astype(BF16)
        mine = ((iota((16, 128), 0) + 1) + m * OWN).astype(F32).astype(BF16)
        for h in range(2):
            lanes = slice(h * 128, h * 128 + 128)
            slots = [spread(slot[o : o + 1, lanes]) for o in range(OBS)]

            def own(value):
                return choose(slots, mine, [spread(value[o : o + 1, lanes]) for o in range(OBS)])

            for a in range(9):
                for b in range(3):
                    zp[a * 16 : a * 16 + 16, b * CAP + h * 128 : b * CAP + h * 128 + 128] = own(
                        z[a, b]
                    )
                for k in range(2):
                    ap[a * 16 : a * 16 + 16, k * CAP + h * 128 : k * CAP + h * 128 + 128] = own(
                        cam[k][a]
                    )
            for k in range(2):
                ap[144:160, k * CAP + h * 128 : k * CAP + h * 128 + 128] = own(res[k])
        acc_u[...] += lax.dot_general(ap[...], ap[0:144, :], NT, preferred_element_type=F32)
        acc_g[...] += lax.dot_general(gp[...], zp[...], NT, preferred_element_type=F32)
        for a in range(9):
            for h in range(2):
                lanes = slice(h * 128, h * 128 + 128)
                slots = [spread(slot[o : o + 1, lanes]) for o in range(OBS)]
                values = [
                    [
                        spread(wv[(a * 3 + b) * 8 + o : (a * 3 + b) * 8 + o + 1, lanes])
                        for o in range(OBS)
                    ]
                    for b in range(3)
                ]
                for t in range(16):
                    here = names + jnp.asarray(16 * t, BF16)
                    outs = [jnp.zeros((16, 128), BF16)] * 3
                    for o in range(OBS):
                        same = slots[o] == here
                        outs = [jnp.where(same, values[b][o], outs[b]) for b in range(3)]
                    for b in range(3):
                        wp[
                            a * CAMS + t * 16 : a * CAMS + t * 16 + 16,
                            b * CAP + h * 128 : b * CAP + h * 128 + 128,
                        ] = outs[b]
            acc[a] += lax.dot_general(
                wp[a * CAMS : (a + 1) * CAMS, :], zp[...], NT, preferred_element_type=F32
            )
        return carry

    lax.fori_loop(0, blocks, chunk, 0)

    rows_u = iota((144, 144), 0)
    cols_u = iota((144, 144), 1)
    block = jnp.where((rows_u & 15) == (cols_u & 15), acc_u[0:144, :], 0.0) + jnp.where(
        rows_u == cols_u, DAMPING, 0.0
    )
    grad = jnp.sum(
        jnp.where(iota((16, 144), 0) == (iota((16, 144), 1) & 15), acc_u[144:160, :], 0.0),
        axis=0,
        keepdims=True,
    ) - jnp.sum(acc_g[...], axis=0, keepdims=True)
    dm[...] = jnp.zeros_like(dm)
    own_rows = pl.ds(pl.multiple_of(m * OWN, OWN), OWN)
    for a in range(9):
        acc[a] = -acc[a]
        acc[a, own_rows, :] += block[a * 16 : a * 16 + 16, :]
        dm[a * 16 : a * 16 + 16, 0:144] = acc[a, own_rows, :]
    dm[144:145, 0:144] = grad
    for a in range(9):
        turned[pl.ds(a, CAMS, stride=9), 0:128] = acc[a, :, 0:128]
        st[pl.ds(a, CAMS, stride=9), :] = jnp.concatenate(
            [acc[a, :, 128:144], jnp.zeros((CAMS, 112), F32)], axis=1
        )
    for t in range(18):
        lanes = slice(t * 128, t * 128 + 128)
        first = turned[lanes, :].T
        for a in range(8):
            woven[pl.ds(t * 144 + a, 16, stride=9), :] = first[a * 16 : a * 16 + 16, :]
        woven[pl.ds(t * 144 + 8, 16, stride=9), :] = st[lanes, :].T[0:16, :]
        out_ref[:, lanes] = woven[t * 144 : t * 144 + 144, :]

    whole = dm[...]
    flipped = whole.T
    lane = iota((144, 256), 1)
    mat = jnp.where(lane < 144, 0.5 * (whole[0:144, :] + flipped[0:144, :]), flipped[0:144, :])
    sub = iota((144, 1), 0)
    left, right = mat[:, 0:128], mat[:, 128:256]
    for k in range(144):
        if k < 128:
            col = left[:, k : k + 1]
        else:
            col = right[:, k - 128 : k - 127]
        scale = 1.0 / col[k : k + 1, :]
        new_right = right[k : k + 1, :] * scale
        less = col - (sub == k).astype(F32)
        if k < 128:
            left = left - less * (left[k : k + 1, :] * scale)
        right = right - less * new_right
    step = jnp.broadcast_to(-right[:, 16:17], (144, 128))
    for a in range(9):
        st[pl.ds(a, 16, stride=9), :] = step[a * 16 : a * 16 + 16, :]
    step_ref[...] = st[0:256, :].T[0:8, :]


def per_device(cam_jac, point_jac, residuals, obs_camera, obs_count, new_cluster, new_slot):
    params = pltpu.CompilerParams(vmem_limit_bytes=VMEM_BYTES)
    vmem = pl.BlockSpec(memory_space=pltpu.VMEM)
    cam = cam_jac.reshape(144, PTS)
    pt = point_jac.reshape(48, PTS)
    res = residuals.reshape(16, PTS)
    slots, far = pl.pallas_call(
        sort_out_kernel,
        out_shape=(jax.ShapeDtypeStruct((16, PTS), BF16), jax.ShapeDtypeStruct((FAR, 256), BF16)),
        in_specs=[vmem] * 7,
        out_specs=(vmem, vmem),
        compiler_params=params,
        name="sort_out",
    )(
        cam,
        pt,
        res,
        obs_camera,
        obs_count.reshape(1, PTS),
        new_cluster.reshape(16, 128),
        new_slot.reshape(16, 128),
    )
    far = lax.all_to_all(
        far.reshape(8, 16, 256), "cluster", split_axis=0, concat_axis=0, tiled=True
    ).reshape(FAR, 256)

    def packed(turn):
        def body(*refs):
            pack_kernel(float(turn * CAP), *refs)

        sent = pl.pallas_call(
            body,
            out_shape=jax.ShapeDtypeStruct((16, ROWS, CAP), BF16),
            in_specs=[vmem] * 5,
            out_specs=vmem,
            scratch_shapes=[pltpu.VMEM((ROWS, ALL), BF16)],
            compiler_params=params,
            name="pack",
        )(cam, pt, res, slots, far)
        return lax.all_to_all(sent, "member", split_axis=0, concat_axis=0, tiled=True)

    def system(blocks):
        count = blocks.shape[0]

        def body(*refs):
            system_kernel(count, *refs)

        return pl.pallas_call(
            body,
            out_shape=(
                jax.ShapeDtypeStruct((144, 9 * CAMS), F32),
                jax.ShapeDtypeStruct((8, 256), F32),
            ),
            in_specs=[pl.BlockSpec(memory_space=pltpu.SMEM), vmem],
            out_specs=(vmem, vmem),
            scratch_shapes=[
                pltpu.VMEM((216, CAP), F32),
                pltpu.VMEM((9 * CAMS, 3 * CAP), BF16),
                pltpu.VMEM((144, 3 * CAP), BF16),
                pltpu.VMEM((160, 2 * CAP), BF16),
                pltpu.VMEM((16, 3 * CAP), BF16),
                pltpu.VMEM((9, CAMS, 144), F32),
                pltpu.VMEM((160, 144), F32),
                pltpu.VMEM((16, 144), F32),
                pltpu.VMEM((9 * CAMS, 128), F32),
                pltpu.VMEM((256, 256), F32),
                pltpu.VMEM((9 * CAMS, 128), F32),
                pltpu.VMEM((18 * 144, 128), F32),
            ],
            compiler_params=params,
            name="system",
        )(lax.axis_index("member").astype(jnp.int32).reshape(1), blocks)

    arrived = packed(0)

    def more_rounds(arrived):
        return system(jnp.concatenate([arrived] + [packed(t) for t in range(1, ROUNDS)], axis=0))

    matrix, step = lax.cond(jnp.max(arrived[:, OVER, 0]) > 0, more_rounds, system, arrived)
    return matrix, step[0, 0:144]


def solution(mesh):
    in_specs = (
        P(None, None, ("cluster", "member")),
        P(None, None, ("cluster", "member")),
        P(None, None, ("cluster", "member")),
        P(None, ("cluster", "member")),
        P(("cluster", "member")),
        P(),
        P(),
    )
    out_specs = (P(("cluster", "member"), None), P(("cluster", "member")))
    return jax.shard_map(
        per_device, mesh=mesh, in_specs=in_specs, out_specs=out_specs, check_vma=False
    )
```

```python
import jax
import jax.numpy as jnp
from jax import lax
from jax.experimental import pallas as pl
from jax.experimental.pallas import tpu as pltpu
from jax.sharding import PartitionSpec as P

CAMS = 256
OWN = 16
OBS = 8
PTS = 512
FAR = 128
ALL = PTS + FAR
CAP = 256
ROWS = 224
SLOT = 208
COUNT = 216
OVER = 217
ROUNDS = -(-ALL // CAP)
DAMPING = 0.5
PIVOT = 8
F32 = jnp.float32
BF16 = jnp.bfloat16
NT = (((1,), (1,)), ((), ()))
VMEM_BYTES = 56 * 1024 * 1024


def iota(shape, dim):
    return lax.broadcasted_iota(jnp.int32, shape, dim)


def running_count(hits):
    tri = (iota((128, 128), 0) <= iota((128, 128), 1)).astype(BF16)
    parts = []
    base = jnp.zeros((hits.shape[0], 1), F32)
    for t in range(hits.shape[1] // 128):
        part = hits[:, t * 128 : (t + 1) * 128]
        parts.append(jnp.dot(part.astype(BF16), tri, preferred_element_type=F32) + base)
        base = base + jnp.sum(part, axis=1, keepdims=True)
    return jnp.concatenate(parts, axis=1)


def sort_out_kernel(cam_ref, pt_ref, res_ref, oc_ref, cnt_ref, ncl_ref, nsl_ref, slot_ref, far_ref):
    ids = oc_ref[...]
    cluster = ids >> 8
    old = cluster[0:1, 0:128]
    code = ncl_ref[...] * CAMS + nsl_ref[...]
    row = iota((16, 128), 0)
    tables = [
        jnp.sum(jnp.where(row == 2 * old + t, code, 0), axis=0, keepdims=True) for t in range(2)
    ]
    tables = [jnp.broadcast_to(t, (OBS, 128)) for t in tables]
    found = []
    for t in range(PTS // 128):
        local = ids[:, t * 128 : (t + 1) * 128] & 255
        lane = local & 127
        low, high = [
            jnp.take_along_axis(table, lane, axis=1, mode="promise_in_bounds") for table in tables
        ]
        found.append(jnp.where(local < 128, low, high))
    found = jnp.concatenate(found, axis=1)
    aim = found >> 8
    place = (found & 255) + 1
    live = iota((OBS, PTS), 0) < cnt_ref[...]
    home = jnp.where(live & (aim == cluster), place, 0)
    abroad = live & (aim != cluster)
    away = jnp.where(abroad, place, 0)
    slot_ref[0:8, :] = home.astype(F32).astype(BF16)
    slot_ref[8:16, :] = jnp.zeros((8, PTS), BF16)
    target = jnp.max(jnp.where(abroad, aim, -1), axis=0, keepdims=True)
    hits = (jnp.broadcast_to(target, (8, PTS)) == iota((8, PTS), 0)).astype(F32)
    rank = jnp.sum((running_count(hits) - 1.0) * hits, axis=0, keepdims=True)
    column = jnp.where(target >= 0, target * 16 + rank.astype(jnp.int32), -1)
    chooser = (jnp.broadcast_to(column, (FAR, PTS)) == iota((FAR, PTS), 0)).astype(BF16)
    mask = abroad.astype(F32)
    mask2 = jnp.concatenate([mask, mask], axis=0).astype(BF16)

    def send(ref, groups):
        rows = jnp.concatenate([ref[16 * g : 16 * g + 16, :] * mask2 for g in range(groups)], axis=0)
        return lax.dot_general(chooser, rows, NT, preferred_element_type=F32)

    far_ref[:, 0:208] = jnp.concatenate(
        [send(cam_ref, 9), send(pt_ref, 3), send(res_ref, 1)], axis=1
    ).astype(BF16)
    slots = jnp.concatenate([away.astype(F32), jnp.zeros((40, PTS), F32)], axis=0).astype(BF16)
    far_ref[:, 208:256] = lax.dot_general(
        chooser, slots, NT, preferred_element_type=F32
    ).astype(BF16)


def pack_kernel(first_rank, cam_ref, pt_ref, res_ref, slot_ref, far_ref, out_ref, feat):
    feat[0:144, 0:PTS] = cam_ref[...]
    feat[144:192, 0:PTS] = pt_ref[...]
    feat[192:208, 0:PTS] = res_ref[...]
    feat[208:224, 0:PTS] = slot_ref[...]
    feat[:, PTS:ALL] = far_ref[...].astype(F32).T[0:ROWS, :].astype(BF16)
    slots = feat[208:224, :].astype(F32)[0:8, :].astype(jnp.int32)
    owner = ((slots + 15) >> 4) - 1
    member = iota((16, ALL), 0)
    touch = jnp.zeros((16, ALL), jnp.bool_)
    for o in range(OBS):
        touch = touch | (jnp.broadcast_to(owner[o : o + 1, :], (16, ALL)) == member)
    hits = touch.astype(F32)
    count = running_count(hits)
    total = jnp.max(count, axis=1, keepdims=True)
    rank = count - 1.0 - first_rank
    rank = jnp.where(touch & (rank >= 0.0) & (rank < CAP), rank, -1.0)
    over = jnp.max((total > CAP).astype(F32), axis=0, keepdims=True)
    seat = iota((CAP, ALL), 0).astype(F32)
    here = jnp.clip(total - first_rank, 0.0, float(CAP))
    line = iota((16, CAP), 0)
    for d in range(16):
        chosen = (jnp.broadcast_to(rank[d : d + 1, :], (CAP, ALL)) == seat).astype(BF16)
        moved = lax.dot_general(feat[...], chosen, NT, preferred_element_type=F32)
        out_ref[d, 0:208, :] = moved[0:208, :].astype(BF16)
        tail = jnp.where(
            line < 8,
            moved[208:224, :],
            jnp.where(line == 8, here[d : d + 1, :], jnp.where(line == 9, over, 0.0)),
        )
        out_ref[d, 208:224, :] = tail.astype(BF16)


def block_values(f):
    slot = f[SLOT : SLOT + 8, :]
    valid = slot > 0.0
    cam = [[f[(k * 9 + a) * 8 : (k * 9 + a) * 8 + 8, :] for a in range(9)] for k in range(2)]
    pt = [
        [
            jnp.where(valid, f[144 + (k * 3 + b) * 8 : 152 + (k * 3 + b) * 8, :], 0.0)
            for b in range(3)
        ]
        for k in range(2)
    ]
    res = [jnp.where(valid, f[192 + k * 8 : 200 + k * 8, :], 0.0) for k in range(2)]

    def over_obs(x):
        return jnp.sum(x, axis=0, keepdims=True)

    v = {}
    for b in range(3):
        for c in range(b, 3):
            v[b, c] = over_obs(pt[0][b] * pt[0][c] + pt[1][b] * pt[1][c]) + (
                DAMPING if b == c else 0.0
            )
            v[c, b] = v[b, c]
    g = [over_obs(pt[0][b] * res[0] + pt[1][b] * res[1]) for b in range(3)]

    def cofactor(i, j):
        r = [x for x in range(3) if x != i]
        c = [x for x in range(3) if x != j]
        minor = v[r[0], c[0]] * v[r[1], c[1]] - v[r[0], c[1]] * v[r[1], c[0]]
        return minor if (i + j) % 2 == 0 else -minor

    cof = {(i, j): cofactor(i, j) for i in range(3) for j in range(i, 3)}
    det = v[0, 0] * cof[0, 0] + v[0, 1] * cof[0, 1] + v[0, 2] * cof[0, 2]
    inv = {}
    for i in range(3):
        for j in range(i, 3):
            inv[i, j] = cof[i, j] / det
            inv[j, i] = inv[i, j]
    w = {}
    z = {}
    for a in range(9):
        for b in range(3):
            w[a, b] = (cam[0][a] * pt[0][b] + cam[1][a] * pt[1][b]).astype(BF16).astype(F32)
        for b in range(3):
            z[a, b] = w[a, 0] * inv[0, b] + w[a, 1] * inv[1, b] + w[a, 2] * inv[2, b]
    return slot, cam, res, w, z, g


def system_kernel(
    blocks, m_ref, count_ref, x_ref, out_ref, step_ref, wv, sv, iv, wp, zp, ap, gp, tiles, acc, acc_u, acc_g, turned, dm, st, woven
):
    m = m_ref[0]
    acc[...] = jnp.zeros_like(acc)
    acc_u[...] = jnp.zeros_like(acc_u)
    acc_g[...] = jnp.zeros_like(acc_g)
    gp[...] = jnp.zeros_like(gp)
    names = (iota((16, 128), 0) + 1).astype(F32).astype(BF16)

    tiles[...] = jnp.zeros_like(tiles)
    lane = iota((ROWS, 128), 1)

    def append(s, used):
        first = used // 128
        shift = used % 128
        two = [
            pltpu.roll(x_ref[s, :, 0:128].astype(F32), shift, 1),
            pltpu.roll(x_ref[s, :, 128:256].astype(F32), shift, 1),
        ]
        tiles[first] += jnp.where(lane >= shift, two[0], 0.0)
        tiles[first + 1] += jnp.where(lane < shift, two[0], two[1])
        tiles[first + 2] += jnp.where(lane < shift, two[1], 0.0)
        return used + count_ref[s]

    used = lax.fori_loop(0, blocks, append, jnp.int32(0))

    def spread(row):
        return jnp.broadcast_to(row, (16, 128)).astype(BF16)

    def seats(slots, own):
        number = jnp.zeros((16, 128), BF16)
        for o in range(OBS):
            number = jnp.where(slots[o] == own, jnp.asarray(o + 1, BF16), number)
        return number

    def split(number):
        index = jnp.maximum(number.astype(F32).astype(jnp.int32) - 1, 0)
        return index[0:8, :], index[8:16, :]

    def seated(value, index, has):
        two = [jnp.take_along_axis(value, i, axis=0, mode="promise_in_bounds") for i in index]
        return jnp.where(has, jnp.concatenate(two, axis=0).astype(BF16), jnp.zeros((16, 128), BF16))

    def chunk(s, carry):
        slot, cam, res, w, z, g = block_values(
            jnp.concatenate([tiles[2 * s], tiles[2 * s + 1]], axis=1)
        )
        for a in range(9):
            for b in range(3):
                wv[(a * 3 + b) * 8 : (a * 3 + b) * 8 + 8, :] = w[a, b]
        for b in range(3):
            high = g[b].astype(BF16)
            rest = g[b] - high.astype(F32)
            mid = rest.astype(BF16)
            low = (rest - mid.astype(F32)).astype(BF16)
            rows = jnp.concatenate(
                [high.astype(F32), mid.astype(F32), low.astype(F32), jnp.zeros((13, CAP), F32)], axis=0
            )
            gp[:, b * CAP : (b + 1) * CAP] = rows.astype(BF16)
        mine = ((iota((16, 128), 0) + 1) + m * OWN).astype(F32).astype(BF16)
        for h in range(2):
            lanes = slice(h * 128, h * 128 + 128)
            slots = [spread(slot[o : o + 1, lanes]) for o in range(OBS)]
            for t in range(16):
                number = seats(slots, names + jnp.asarray(16 * t, BF16))
                low, high = split(number)
                sv[t * 16 : t * 16 + 16, lanes] = number
                iv[t * 16 : t * 16 + 8, lanes] = low
                iv[t * 16 + 8 : t * 16 + 16, lanes] = high
            number = seats(slots, mine)
            index = split(number)
            has = number > 0

            def own(value):
                return seated(value[:, lanes], index, has)

            for a in range(9):
                for b in range(3):
                    zp[a * 16 : a * 16 + 16, b * CAP + h * 128 : b * CAP + h * 128 + 128] = own(
                        z[a, b]
                    )
                for k in range(2):
                    ap[a * 16 : a * 16 + 16, k * CAP + h * 128 : k * CAP + h * 128 + 128] = own(
                        cam[k][a]
                    )
            for k in range(2):
                ap[144:160, k * CAP + h * 128 : k * CAP + h * 128 + 128] = own(res[k])
        acc_u[...] += lax.dot_general(ap[...], ap[0:144, :], NT, preferred_element_type=F32)
        acc_g[...] += lax.dot_general(gp[...], zp[...], NT, preferred_element_type=F32)
        for a in range(9):
            for h in range(2):
                lanes = slice(h * 128, h * 128 + 128)
                values = [wv[(a * 3 + b) * 8 : (a * 3 + b) * 8 + 8, lanes] for b in range(3)]
                for t in range(16):
                    has = sv[t * 16 : t * 16 + 16, lanes] > 0
                    index = (iv[t * 16 : t * 16 + 8, lanes], iv[t * 16 + 8 : t * 16 + 16, lanes])
                    for b in range(3):
                        wp[
                            a * CAMS + t * 16 : a * CAMS + t * 16 + 16,
                            b * CAP + h * 128 : b * CAP + h * 128 + 128,
                        ] = seated(values[b], index, has)
            if a % 3 == 2:
                three = lax.dot_general(
                    wp[(a - 2) * CAMS : (a + 1) * CAMS, :], zp[...], NT, preferred_element_type=F32
                )
                for q in range(3):
                    acc[a - 2 + q] += three[q * CAMS : (q + 1) * CAMS, :]
        return carry

    lax.fori_loop(0, (used + CAP - 1) // CAP, chunk, 0)

    rows_u = iota((144, 144), 0)
    cols_u = iota((144, 144), 1)
    block = jnp.where((rows_u & 15) == (cols_u & 15), acc_u[0:144, :], 0.0) + jnp.where(
        rows_u == cols_u, DAMPING, 0.0
    )
    grad = jnp.sum(
        jnp.where(iota((16, 144), 0) == (iota((16, 144), 1) & 15), acc_u[144:160, :], 0.0),
        axis=0,
        keepdims=True,
    ) - jnp.sum(acc_g[...], axis=0, keepdims=True)
    dm[...] = jnp.zeros_like(dm)
    own_rows = pl.ds(pl.multiple_of(m * OWN, OWN), OWN)
    for a in range(9):
        acc[a] = -acc[a]
        acc[a, own_rows, :] += block[a * 16 : a * 16 + 16, :]
        dm[a * 16 : a * 16 + 16, 0:144] = acc[a, own_rows, :]
    dm[144:145, 0:144] = grad
    for a in range(9):
        turned[pl.ds(a, CAMS, stride=9), 0:128] = acc[a, :, 0:128]
        st[pl.ds(a, CAMS, stride=9), :] = jnp.concatenate(
            [acc[a, :, 128:144], jnp.zeros((CAMS, 112), F32)], axis=1
        )

    def weave(t):
        lanes = slice(t * 128, t * 128 + 128)
        first = turned[lanes, :].T
        for a in range(8):
            woven[pl.ds(t * 144 + a, 16, stride=9), :] = first[a * 16 : a * 16 + 16, :]
        woven[pl.ds(t * 144 + 8, 16, stride=9), :] = st[lanes, :].T[0:16, :]
        out_ref[:, lanes] = woven[t * 144 : t * 144 + 144, :]

    whole = dm[...]
    flipped = whole.T
    here = iota((8, 256), 1)
    left, right = [], []
    for i in range(18):
        rows = slice(i * 8, i * 8 + 8)
        tile = jnp.where(here < 144, 0.5 * (whole[rows, :] + flipped[rows, :]), flipped[rows, :])
        left.append(tile[:, 0:128])
        right.append(tile[:, 128:256])
    sub = iota((8, 128), 0)
    for k in range(0, 144, PIVOT):
        top = k // 8
        both = k < 128
        cols = []
        for q in range(PIVOT):
            half, c = (left, k + q) if both else (right, k + q - 128)
            cols.append([jnp.broadcast_to(half[i][:, c : c + 1], (8, 128)) for i in range(18)])

        def row_of(tile, q):
            r = (k + q) % 8
            return jnp.broadcast_to(tile[r : r + 1, :], (8, 128))

        piv = [[row_of(cols[j][top], q) for j in range(PIVOT)] for q in range(PIVOT)]
        rhs = [
            ([row_of(left[top], q)] if both else []) + [row_of(right[top], q)] for q in range(PIVOT)
        ]
        for q in range(PIVOT):
            guess = pl.reciprocal(piv[q][q], approx=True)
            for _ in range(2):
                guess = guess * (2.0 - piv[q][q] * guess)
            for j in range(q + 1, PIVOT):
                piv[q][j] = piv[q][j] * guess
            rhs[q] = [v * guess for v in rhs[q]]
            for r in range(PIVOT):
                if r != q:
                    for j in range(q + 1, PIVOT):
                        piv[r][j] = piv[r][j] - piv[r][q] * piv[q][j]
                    rhs[r] = [v - piv[r][q] * n for v, n in zip(rhs[r], rhs[q])]
        for i in range(18):
            for q in range(PIVOT):
                less = cols[q][i]
                if i == top:
                    less = less - (sub == (k + q) % 8).astype(F32)
                if both:
                    left[i] = left[i] - less * rhs[q][0]
                right[i] = right[i] - less * rhs[q][-1]
        if k % 8 == 0:
            weave(k // 8)
    for i in range(18):
        woven[i * 8 : i * 8 + 8, :] = jnp.broadcast_to(-right[i][:, 16:17], (8, 128))
    for a in range(9):
        st[pl.ds(a, 16, stride=9), :] = woven[a * 16 : a * 16 + 16, :]
    step_ref[...] = st[0:256, :].T[0:8, :]


def per_device(cam_jac, point_jac, residuals, obs_camera, obs_count, new_cluster, new_slot):
    params = pltpu.CompilerParams(vmem_limit_bytes=VMEM_BYTES)
    vmem = pl.BlockSpec(memory_space=pltpu.VMEM)
    cam = cam_jac.reshape(144, PTS)
    pt = point_jac.reshape(48, PTS)
    res = residuals.reshape(16, PTS)
    slots, far = pl.pallas_call(
        sort_out_kernel,
        out_shape=(jax.ShapeDtypeStruct((16, PTS), BF16), jax.ShapeDtypeStruct((FAR, 256), BF16)),
        in_specs=[vmem] * 7,
        out_specs=(vmem, vmem),
        compiler_params=params,
        name="sort_out",
    )(
        cam,
        pt,
        res,
        obs_camera,
        obs_count.reshape(1, PTS),
        new_cluster.reshape(16, 128),
        new_slot.reshape(16, 128),
    )
    far = lax.all_to_all(
        far.reshape(8, 16, 256), "cluster", split_axis=0, concat_axis=0, tiled=True
    ).reshape(FAR, 256)

    def packed(turn):
        def body(*refs):
            pack_kernel(float(turn * CAP), *refs)

        sent = pl.pallas_call(
            body,
            out_shape=jax.ShapeDtypeStruct((16, ROWS, CAP), BF16),
            in_specs=[vmem] * 5,
            out_specs=vmem,
            scratch_shapes=[pltpu.VMEM((ROWS, ALL), BF16)],
            compiler_params=params,
            name="pack",
        )(cam, pt, res, slots, far)
        return lax.all_to_all(sent, "member", split_axis=0, concat_axis=0, tiled=True)

    def system(blocks):
        count = blocks.shape[0]
        counts = blocks[:, COUNT, 0].astype(jnp.int32)

        def body(*refs):
            system_kernel(count, *refs)

        return pl.pallas_call(
            body,
            out_shape=(
                jax.ShapeDtypeStruct((144, 9 * CAMS), F32),
                jax.ShapeDtypeStruct((8, 256), F32),
            ),
            in_specs=[pl.BlockSpec(memory_space=pltpu.SMEM)] * 2 + [vmem],
            out_specs=(vmem, vmem),
            scratch_shapes=[
                pltpu.VMEM((216, CAP), F32),
                pltpu.VMEM((CAMS, CAP), BF16),
                pltpu.VMEM((CAMS, CAP), jnp.int32),
                pltpu.VMEM((9 * CAMS, 3 * CAP), BF16),
                pltpu.VMEM((144, 3 * CAP), BF16),
                pltpu.VMEM((160, 2 * CAP), BF16),
                pltpu.VMEM((16, 3 * CAP), BF16),
                pltpu.VMEM((2 * count + 2, ROWS, 128), F32),
                pltpu.VMEM((9, CAMS, 144), F32),
                pltpu.VMEM((160, 144), F32),
                pltpu.VMEM((16, 144), F32),
                pltpu.VMEM((9 * CAMS, 128), F32),
                pltpu.VMEM((256, 256), F32),
                pltpu.VMEM((9 * CAMS, 128), F32),
                pltpu.VMEM((18 * 144, 128), F32),
            ],
            compiler_params=params,
            name="system",
        )(lax.axis_index("member").astype(jnp.int32).reshape(1), counts, blocks)

    arrived = packed(0)

    def more_rounds(arrived):
        return system(jnp.concatenate([arrived] + [packed(t) for t in range(1, ROUNDS)], axis=0))

    matrix, step = lax.cond(jnp.max(arrived[:, OVER, 0]) > 0, more_rounds, system, arrived)
    return matrix, step[0, 0:144]


def solution(mesh):
    in_specs = (
        P(None, None, ("cluster", "member")),
        P(None, None, ("cluster", "member")),
        P(None, None, ("cluster", "member")),
        P(None, ("cluster", "member")),
        P(("cluster", "member")),
        P(),
        P(),
    )
    out_specs = (P(("cluster", "member"), None), P(("cluster", "member")))
    return jax.shard_map(
        per_device, mesh=mesh, in_specs=in_specs, out_specs=out_specs, check_vma=False
    )
```

```python
import jax
import jax.numpy as jnp
from jax import lax
from jax.experimental import pallas as pl
from jax.experimental.pallas import tpu as pltpu
from jax.sharding import PartitionSpec as P

CAMS = 256
OWN = 16
OBS = 8
PTS = 512
FAR = 128
ALL = PTS + FAR
CAP = 256
ROWS = 224
SLOT = 208
COUNT = 216
OVER = 217
ROUNDS = -(-ALL // CAP)
DAMPING = 0.5
PIVOT = 8
F32 = jnp.float32
BF16 = jnp.bfloat16
ALONG_ROWS = lax.GatherDimensionNumbers(
    offset_dims=(),
    collapsed_slice_dims=(0,),
    start_index_map=(0,),
    operand_batching_dims=(1,),
    start_indices_batching_dims=(1,),
)
NT = (((1,), (1,)), ((), ()))
VMEM_BYTES = 56 * 1024 * 1024


def iota(shape, dim):
    return lax.broadcasted_iota(jnp.int32, shape, dim)


def running_count(hits):
    tri = (iota((128, 128), 0) <= iota((128, 128), 1)).astype(BF16)
    parts = []
    base = jnp.zeros((hits.shape[0], 1), F32)
    for t in range(hits.shape[1] // 128):
        part = hits[:, t * 128 : (t + 1) * 128]
        parts.append(jnp.dot(part.astype(BF16), tri, preferred_element_type=F32) + base)
        base = base + jnp.sum(part, axis=1, keepdims=True)
    return jnp.concatenate(parts, axis=1)


def sort_out_kernel(cam_ref, pt_ref, res_ref, oc_ref, cnt_ref, ncl_ref, nsl_ref, slot_ref, far_ref):
    ids = oc_ref[...]
    cluster = ids >> 8
    old = cluster[0:1, 0:128]
    code = ncl_ref[...] * CAMS + nsl_ref[...]
    row = iota((16, 128), 0)
    tables = [
        jnp.sum(jnp.where(row == 2 * old + t, code, 0), axis=0, keepdims=True) for t in range(2)
    ]
    tables = [jnp.broadcast_to(t, (OBS, 128)) for t in tables]
    found = []
    for t in range(PTS // 128):
        local = ids[:, t * 128 : (t + 1) * 128] & 255
        lane = local & 127
        low, high = [
            jnp.take_along_axis(table, lane, axis=1, mode="promise_in_bounds") for table in tables
        ]
        found.append(jnp.where(local < 128, low, high))
    found = jnp.concatenate(found, axis=1)
    aim = found >> 8
    place = (found & 255) + 1
    live = iota((OBS, PTS), 0) < cnt_ref[...]
    home = jnp.where(live & (aim == cluster), place, 0)
    abroad = live & (aim != cluster)
    away = jnp.where(abroad, place, 0)
    slot_ref[0:8, :] = home.astype(F32).astype(BF16)
    slot_ref[8:16, :] = jnp.zeros((8, PTS), BF16)
    target = jnp.max(jnp.where(abroad, aim, -1), axis=0, keepdims=True)
    hits = (jnp.broadcast_to(target, (8, PTS)) == iota((8, PTS), 0)).astype(F32)
    rank = jnp.sum((running_count(hits) - 1.0) * hits, axis=0, keepdims=True)
    column = jnp.where(target >= 0, target * 16 + rank.astype(jnp.int32), -1)
    chooser = (jnp.broadcast_to(column, (FAR, PTS)) == iota((FAR, PTS), 0)).astype(BF16)
    mask = abroad.astype(F32)
    mask2 = jnp.concatenate([mask, mask], axis=0).astype(BF16)

    def send(ref, groups):
        rows = jnp.concatenate([ref[16 * g : 16 * g + 16, :] * mask2 for g in range(groups)], axis=0)
        return lax.dot_general(chooser, rows, NT, preferred_element_type=F32)

    far_ref[:, 0:208] = jnp.concatenate(
        [send(cam_ref, 9), send(pt_ref, 3), send(res_ref, 1)], axis=1
    ).astype(BF16)
    slots = jnp.concatenate([away.astype(F32), jnp.zeros((40, PTS), F32)], axis=0).astype(BF16)
    far_ref[:, 208:256] = lax.dot_general(
        chooser, slots, NT, preferred_element_type=F32
    ).astype(BF16)


def pack_kernel(first_rank, cam_ref, pt_ref, res_ref, slot_ref, far_ref, out_ref, feat):
    feat[0:144, 0:PTS] = cam_ref[...]
    feat[144:192, 0:PTS] = pt_ref[...]
    feat[192:208, 0:PTS] = res_ref[...]
    feat[208:224, 0:PTS] = slot_ref[...]
    feat[:, PTS:ALL] = far_ref[...].astype(F32).T[0:ROWS, :].astype(BF16)
    slots = feat[208:224, :].astype(F32)[0:8, :].astype(jnp.int32)
    owner = ((slots + 15) >> 4) - 1
    member = iota((16, ALL), 0)
    touch = jnp.zeros((16, ALL), jnp.bool_)
    for o in range(OBS):
        touch = touch | (jnp.broadcast_to(owner[o : o + 1, :], (16, ALL)) == member)
    hits = touch.astype(F32)
    count = running_count(hits)
    total = jnp.max(count, axis=1, keepdims=True)
    rank = count - 1.0 - first_rank
    rank = jnp.where(touch & (rank >= 0.0) & (rank < CAP), rank, -1.0)
    over = jnp.max((total > CAP).astype(F32), axis=0, keepdims=True)
    seat = iota((CAP, ALL), 0).astype(F32).astype(BF16)
    here = jnp.clip(total - first_rank, 0.0, float(CAP))
    line = iota((16, CAP), 0)
    for d in range(16):
        asked = jnp.broadcast_to(rank[d : d + 1, :], (16, ALL)).astype(BF16)
        asked = jnp.concatenate([asked] * (CAP // 16), axis=0)
        chosen = jnp.where(asked == seat, jnp.asarray(1, BF16), jnp.asarray(0, BF16))
        moved = lax.dot_general(feat[...], chosen, NT, preferred_element_type=F32)
        out_ref[d, 0:208, :] = moved[0:208, :].astype(BF16)
        tail = jnp.where(
            line < 8,
            moved[208:224, :],
            jnp.where(line == 8, here[d : d + 1, :], jnp.where(line == 9, over, 0.0)),
        )
        out_ref[d, 208:224, :] = tail.astype(BF16)


def block_values(f):
    slot = f[SLOT : SLOT + 8, :]
    valid = slot > 0.0
    cam = [[f[(k * 9 + a) * 8 : (k * 9 + a) * 8 + 8, :] for a in range(9)] for k in range(2)]
    pt = [
        [
            jnp.where(valid, f[144 + (k * 3 + b) * 8 : 152 + (k * 3 + b) * 8, :], 0.0)
            for b in range(3)
        ]
        for k in range(2)
    ]
    res = [jnp.where(valid, f[192 + k * 8 : 200 + k * 8, :], 0.0) for k in range(2)]

    def over_obs(x):
        return jnp.sum(x, axis=0, keepdims=True)

    v = {}
    for b in range(3):
        for c in range(b, 3):
            v[b, c] = over_obs(pt[0][b] * pt[0][c] + pt[1][b] * pt[1][c]) + (
                DAMPING if b == c else 0.0
            )
            v[c, b] = v[b, c]
    g = [over_obs(pt[0][b] * res[0] + pt[1][b] * res[1]) for b in range(3)]

    def cofactor(i, j):
        r = [x for x in range(3) if x != i]
        c = [x for x in range(3) if x != j]
        minor = v[r[0], c[0]] * v[r[1], c[1]] - v[r[0], c[1]] * v[r[1], c[0]]
        return minor if (i + j) % 2 == 0 else -minor

    cof = {(i, j): cofactor(i, j) for i in range(3) for j in range(i, 3)}
    det = v[0, 0] * cof[0, 0] + v[0, 1] * cof[0, 1] + v[0, 2] * cof[0, 2]
    inv = {}
    for i in range(3):
        for j in range(i, 3):
            inv[i, j] = cof[i, j] / det
            inv[j, i] = inv[i, j]
    w = {}
    z = {}
    for a in range(9):
        for b in range(3):
            w[a, b] = (cam[0][a] * pt[0][b] + cam[1][a] * pt[1][b]).astype(BF16).astype(F32)
        for b in range(3):
            z[a, b] = w[a, 0] * inv[0, b] + w[a, 1] * inv[1, b] + w[a, 2] * inv[2, b]
    return slot, cam, res, w, z, g


def system_kernel(
    blocks, m_ref, x_ref, out_ref, step_ref, wv, iv, wp, zp, ap, gp, tiles, acc, acc_u, acc_g, turned, dm, st, woven, counts
):
    m = m_ref[0]
    acc[...] = jnp.zeros_like(acc)
    acc_u[...] = jnp.zeros_like(acc_u)
    acc_g[...] = jnp.zeros_like(acc_g)
    gp[...] = jnp.zeros_like(gp)
    names = (iota((16, 128), 0) + 1).astype(F32).astype(BF16)

    lane = iota((ROWS, 128), 1)
    place = (iota((16, 128), 0) == COUNT - SLOT) & (iota((16, 128), 1) == 0)
    for s in range(blocks):
        line = x_ref[s, SLOT:ROWS, 0:128].astype(F32)
        counts[s] = jnp.sum(jnp.where(place, line, 0.0)).astype(jnp.int32)

    def append(s, used):
        first = used // 128
        shift = used % 128
        two = [
            pltpu.roll(x_ref[s, :, 0:128].astype(F32), shift, 1),
            pltpu.roll(x_ref[s, :, 128:256].astype(F32), shift, 1),
        ]
        tiles[first] = jnp.where(lane >= shift, two[0], tiles[first])
        tiles[first + 1] = jnp.where(lane < shift, two[0], two[1])
        tiles[first + 2] = jnp.where(lane < shift, two[1], 0.0)
        return used + counts[s]

    tiles[0] = jnp.zeros((ROWS, 128), F32)
    used = lax.fori_loop(0, blocks, append, jnp.int32(0))
    tiles[used // 128 + 1] = jnp.zeros((ROWS, 128), F32)

    def spread(row):
        return jnp.broadcast_to(row, (16, 128)).astype(BF16)

    def seats(slots, own):
        number = jnp.full((16, 128), 8, jnp.int16)
        for o in range(OBS):
            number = jnp.where(slots[o] == own, jnp.int16(o), number)
        return number

    def table(value):
        return jnp.concatenate([value, jnp.zeros_like(value)], axis=0).astype(BF16)

    def seated(values, index):
        return lax.gather(
            values, index[..., None], ALONG_ROWS, (1, 1), mode=lax.GatherScatterMode.PROMISE_IN_BOUNDS
        )

    def chunk(s, carry):
        slot, cam, res, w, z, g = block_values(
            jnp.concatenate([tiles[2 * s], tiles[2 * s + 1]], axis=1)
        )
        for a in range(9):
            for b in range(3):
                wv[(a * 3 + b) * 16 : (a * 3 + b) * 16 + 16, :] = table(w[a, b])
        for b in range(3):
            high = g[b].astype(BF16)
            rest = g[b] - high.astype(F32)
            mid = rest.astype(BF16)
            low = (rest - mid.astype(F32)).astype(BF16)
            rows = jnp.concatenate(
                [high.astype(F32), mid.astype(F32), low.astype(F32), jnp.zeros((13, CAP), F32)], axis=0
            )
            gp[:, b * CAP : (b + 1) * CAP] = rows.astype(BF16)
        mine = ((iota((16, 128), 0) + 1) + m * OWN).astype(F32).astype(BF16)
        for h in range(2):
            lanes = slice(h * 128, h * 128 + 128)
            slots = [spread(slot[o : o + 1, lanes]) for o in range(OBS)]
            for t in range(16):
                iv[t * 16 : t * 16 + 16, lanes] = seats(slots, names + jnp.asarray(16 * t, BF16))
            index = seats(slots, mine)

            def own(value):
                return seated(table(value[:, lanes]), index)

            for a in range(9):
                for b in range(3):
                    zp[a * 16 : a * 16 + 16, b * CAP + h * 128 : b * CAP + h * 128 + 128] = own(
                        z[a, b]
                    )
                for k in range(2):
                    ap[a * 16 : a * 16 + 16, k * CAP + h * 128 : k * CAP + h * 128 + 128] = own(
                        cam[k][a]
                    )
            for k in range(2):
                ap[144:160, k * CAP + h * 128 : k * CAP + h * 128 + 128] = own(res[k])
        acc_u[...] += lax.dot_general(ap[...], ap[0:144, :], NT, preferred_element_type=F32)
        acc_g[...] += lax.dot_general(gp[...], zp[...], NT, preferred_element_type=F32)
        for a in range(9):
            for h in range(2):
                lanes = slice(h * 128, h * 128 + 128)
                values = [wv[(a * 3 + b) * 16 : (a * 3 + b) * 16 + 16, lanes] for b in range(3)]
                for t in range(16):
                    index = iv[t * 16 : t * 16 + 16, lanes]
                    for b in range(3):
                        wp[
                            a * CAMS + t * 16 : a * CAMS + t * 16 + 16,
                            b * CAP + h * 128 : b * CAP + h * 128 + 128,
                        ] = seated(values[b], index)
            if a % 3 == 2:
                three = lax.dot_general(
                    wp[(a - 2) * CAMS : (a + 1) * CAMS, :], zp[...], NT, preferred_element_type=F32
                )
                for q in range(3):
                    acc[a - 2 + q] += three[q * CAMS : (q + 1) * CAMS, :]
        return carry

    lax.fori_loop(0, (used + CAP - 1) // CAP, chunk, 0)

    rows_u = iota((144, 144), 0)
    cols_u = iota((144, 144), 1)
    block = jnp.where((rows_u & 15) == (cols_u & 15), acc_u[0:144, :], 0.0) + jnp.where(
        rows_u == cols_u, DAMPING, 0.0
    )
    grad = jnp.sum(
        jnp.where(iota((16, 144), 0) == (iota((16, 144), 1) & 15), acc_u[144:160, :], 0.0),
        axis=0,
        keepdims=True,
    ) - jnp.sum(acc_g[...], axis=0, keepdims=True)
    dm[...] = jnp.zeros_like(dm)
    own_rows = pl.ds(pl.multiple_of(m * OWN, OWN), OWN)
    for a in range(9):
        acc[a] = -acc[a]
        acc[a, own_rows, :] += block[a * 16 : a * 16 + 16, :]
        dm[a * 16 : a * 16 + 16, 0:144] = acc[a, own_rows, :]
    dm[144:145, 0:144] = grad
    for a in range(9):
        turned[pl.ds(a, CAMS, stride=9), 0:128] = acc[a, :, 0:128]
        st[pl.ds(a, CAMS, stride=9), :] = jnp.concatenate(
            [acc[a, :, 128:144], jnp.zeros((CAMS, 112), F32)], axis=1
        )

    def weave(t):
        lanes = slice(t * 128, t * 128 + 128)
        first = turned[lanes, :].T
        for a in range(8):
            woven[pl.ds(t * 144 + a, 16, stride=9), :] = first[a * 16 : a * 16 + 16, :]
        woven[pl.ds(t * 144 + 8, 16, stride=9), :] = st[lanes, :].T[0:16, :]
        out_ref[:, lanes] = woven[t * 144 : t * 144 + 144, :]

    whole = dm[...]
    flipped = whole.T
    here = iota((8, 256), 1)
    left, right = [], []
    for i in range(18):
        rows = slice(i * 8, i * 8 + 8)
        tile = jnp.where(here < 144, 0.5 * (whole[rows, :] + flipped[rows, :]), flipped[rows, :])
        left.append(tile[:, 0:128])
        right.append(tile[:, 128:256])
    sub = iota((8, 128), 0)
    for k in range(0, 144, PIVOT):
        top = k // 8
        both = k < 128
        cols = []
        for q in range(PIVOT):
            half, c = (left, k + q) if both else (right, k + q - 128)
            cols.append([jnp.broadcast_to(half[i][:, c : c + 1], (8, 128)) for i in range(18)])

        def row_of(tile, q):
            r = (k + q) % 8
            return jnp.broadcast_to(tile[r : r + 1, :], (8, 128))

        piv = [[row_of(cols[j][top], q) for j in range(PIVOT)] for q in range(PIVOT)]
        rhs = [
            ([row_of(left[top], q)] if both else []) + [row_of(right[top], q)] for q in range(PIVOT)
        ]
        for q in range(0, PIVOT, 2):
            a, b, c, d = piv[q][q], piv[q][q + 1], piv[q + 1][q], piv[q + 1][q + 1]
            det = a * d - b * c
            guess = pl.reciprocal(det, approx=True)
            for _ in range(2):
                guess = guess * (2.0 - det * guess)
            ia, ib, ic, id_ = d * guess, b * guess, c * guess, a * guess
            top_two = [piv[q][q + 2 :] + rhs[q], piv[q + 1][q + 2 :] + rhs[q + 1]]
            new = [
                [ia * u - ib * v for u, v in zip(*top_two)],
                [id_ * v - ic * u for u, v in zip(*top_two)],
            ]
            left_over = PIVOT - q - 2
            for r in range(PIVOT):
                if r in (q, q + 1):
                    rest = new[r - q]
                else:
                    rest = [
                        w - piv[r][q] * u - piv[r][q + 1] * v
                        for w, u, v in zip(piv[r][q + 2 :] + rhs[r], *new)
                    ]
                piv[r] = piv[r][: q + 2] + rest[:left_over]
                rhs[r] = rest[left_over:]
        for i in range(18):
            for q in range(PIVOT):
                less = cols[q][i]
                if i == top:
                    less = less - (sub == (k + q) % 8).astype(F32)
                if both:
                    left[i] = left[i] - less * rhs[q][0]
                right[i] = right[i] - less * rhs[q][-1]
        if k % 8 == 0:
            weave(k // 8)
    for i in range(18):
        woven[i * 8 : i * 8 + 8, :] = jnp.broadcast_to(-right[i][:, 16:17], (8, 128))
    for a in range(9):
        st[pl.ds(a, 16, stride=9), :] = woven[a * 16 : a * 16 + 16, :]
    step_ref[...] = st[0:256, :].T[0, 0:144]


def per_device(cam_jac, point_jac, residuals, obs_camera, obs_count, new_cluster, new_slot):
    params = pltpu.CompilerParams(vmem_limit_bytes=VMEM_BYTES)
    vmem = pl.BlockSpec(memory_space=pltpu.VMEM)
    cam = cam_jac.reshape(144, PTS)
    pt = point_jac.reshape(48, PTS)
    res = residuals.reshape(16, PTS)
    slots, far = pl.pallas_call(
        sort_out_kernel,
        out_shape=(jax.ShapeDtypeStruct((16, PTS), BF16), jax.ShapeDtypeStruct((FAR, 256), BF16)),
        in_specs=[vmem] * 7,
        out_specs=(vmem, vmem),
        compiler_params=params,
        name="sort_out",
    )(
        cam,
        pt,
        res,
        obs_camera,
        obs_count.reshape(1, PTS),
        new_cluster.reshape(16, 128),
        new_slot.reshape(16, 128),
    )
    far = lax.all_to_all(
        far.reshape(8, 16, 256), "cluster", split_axis=0, concat_axis=0, tiled=True
    ).reshape(FAR, 256)

    def packed(turn):
        def body(*refs):
            pack_kernel(float(turn * CAP), *refs)

        sent = pl.pallas_call(
            body,
            out_shape=jax.ShapeDtypeStruct((16, ROWS, CAP), BF16),
            in_specs=[vmem] * 5,
            out_specs=vmem,
            scratch_shapes=[pltpu.VMEM((ROWS, ALL), BF16)],
            compiler_params=params,
            name="pack",
        )(cam, pt, res, slots, far)
        return lax.all_to_all(sent, "member", split_axis=0, concat_axis=0, tiled=True)

    def system(blocks):
        count = blocks.shape[0]

        def body(*refs):
            system_kernel(count, *refs)

        return pl.pallas_call(
            body,
            out_shape=(
                jax.ShapeDtypeStruct((144, 9 * CAMS), F32),
                jax.ShapeDtypeStruct((144,), F32),
            ),
            in_specs=[pl.BlockSpec(memory_space=pltpu.SMEM), vmem],
            out_specs=(vmem, vmem),
            scratch_shapes=[
                pltpu.VMEM((432, CAP), BF16),
                pltpu.VMEM((CAMS, CAP), jnp.int16),
                pltpu.VMEM((9 * CAMS, 3 * CAP), BF16),
                pltpu.VMEM((144, 3 * CAP), BF16),
                pltpu.VMEM((160, 2 * CAP), BF16),
                pltpu.VMEM((16, 3 * CAP), BF16),
                pltpu.VMEM((2 * count + 2, ROWS, 128), F32),
                pltpu.VMEM((9, CAMS, 144), F32),
                pltpu.VMEM((160, 144), F32),
                pltpu.VMEM((16, 144), F32),
                pltpu.VMEM((9 * CAMS, 128), F32),
                pltpu.VMEM((256, 256), F32),
                pltpu.VMEM((9 * CAMS, 128), F32),
                pltpu.VMEM((18 * 144, 128), F32),
                pltpu.SMEM((count,), jnp.int32),
            ],
            compiler_params=params,
            name="system",
        )(lax.axis_index("member").astype(jnp.int32).reshape(1), blocks)

    arrived = packed(0)

    def more_rounds(arrived):
        return system(jnp.concatenate([arrived] + [packed(t) for t in range(1, ROUNDS)], axis=0))

    matrix, step = lax.cond(jnp.max(arrived[:, OVER, 0]) > 0, more_rounds, system, arrived)
    return matrix, step


def solution(mesh):
    in_specs = (
        P(None, None, ("cluster", "member")),
        P(None, None, ("cluster", "member")),
        P(None, None, ("cluster", "member")),
        P(None, ("cluster", "member")),
        P(("cluster", "member")),
        P(),
        P(),
    )
    out_specs = (P(("cluster", "member"), None), P(("cluster", "member")))
    return jax.shard_map(
        per_device, mesh=mesh, in_specs=in_specs, out_specs=out_specs, check_vma=False
    )
```

```python
import jax
import jax.numpy as jnp
from jax import lax
from jax.experimental import pallas as pl
from jax.experimental.pallas import tpu as pltpu
from jax.sharding import PartitionSpec as P

CAMS = 256
OWN = 16
OBS = 8
PTS = 512
FAR = 128
ALL = PTS + FAR
CAP = 256
ROWS = 224
SLOT = 208
COUNT = 216
OVER = 217
ROUNDS = -(-ALL // CAP)
DAMPING = 0.5
PIVOT = 8
STEP = 16
F32 = jnp.float32
BF16 = jnp.bfloat16
ALONG_ROWS = lax.GatherDimensionNumbers(
    offset_dims=(),
    collapsed_slice_dims=(0,),
    start_index_map=(0,),
    operand_batching_dims=(1,),
    start_indices_batching_dims=(1,),
)
NT = (((1,), (1,)), ((), ()))
VMEM_BYTES = 56 * 1024 * 1024


def iota(shape, dim):
    return lax.broadcasted_iota(jnp.int32, shape, dim)


def running_count(hits):
    tri = (iota((128, 128), 0) <= iota((128, 128), 1)).astype(BF16)
    parts = []
    base = jnp.zeros((hits.shape[0], 1), F32)
    for t in range(hits.shape[1] // 128):
        part = hits[:, t * 128 : (t + 1) * 128]
        parts.append(jnp.dot(part.astype(BF16), tri, preferred_element_type=F32) + base)
        base = base + jnp.sum(part, axis=1, keepdims=True)
    return jnp.concatenate(parts, axis=1)


def sort_out_kernel(cam_ref, pt_ref, res_ref, oc_ref, cnt_ref, ncl_ref, nsl_ref, slot_ref, far_ref):
    ids = oc_ref[...]
    cluster = ids >> 8
    old = cluster[0:1, 0:128]
    code = ncl_ref[...] * CAMS + nsl_ref[...]
    row = iota((16, 128), 0)
    tables = [
        jnp.sum(jnp.where(row == 2 * old + t, code, 0), axis=0, keepdims=True) for t in range(2)
    ]
    tables = [jnp.broadcast_to(t, (OBS, 128)) for t in tables]
    found = []
    for t in range(PTS // 128):
        local = ids[:, t * 128 : (t + 1) * 128] & 255
        lane = local & 127
        low, high = [
            jnp.take_along_axis(table, lane, axis=1, mode="promise_in_bounds") for table in tables
        ]
        found.append(jnp.where(local < 128, low, high))
    found = jnp.concatenate(found, axis=1)
    aim = found >> 8
    place = (found & 255) + 1
    live = iota((OBS, PTS), 0) < cnt_ref[...]
    home = jnp.where(live & (aim == cluster), place, 0)
    abroad = live & (aim != cluster)
    away = jnp.where(abroad, place, 0)
    slot_ref[0:8, :] = home.astype(F32).astype(BF16)
    slot_ref[8:16, :] = jnp.zeros((8, PTS), BF16)
    target = jnp.max(jnp.where(abroad, aim, -1), axis=0, keepdims=True)
    hits = (jnp.broadcast_to(target, (8, PTS)) == iota((8, PTS), 0)).astype(F32)
    rank = jnp.sum((running_count(hits) - 1.0) * hits, axis=0, keepdims=True)
    column = jnp.where(target >= 0, target * 16 + rank.astype(jnp.int32), -1)
    chooser = (jnp.broadcast_to(column, (FAR, PTS)) == iota((FAR, PTS), 0)).astype(BF16)
    mask = abroad.astype(F32)
    mask2 = jnp.concatenate([mask, mask], axis=0).astype(BF16)

    def send(ref, groups):
        rows = jnp.concatenate([ref[16 * g : 16 * g + 16, :] * mask2 for g in range(groups)], axis=0)
        return lax.dot_general(chooser, rows, NT, preferred_element_type=F32)

    far_ref[:, 0:208] = jnp.concatenate(
        [send(cam_ref, 9), send(pt_ref, 3), send(res_ref, 1)], axis=1
    ).astype(BF16)
    slots = jnp.concatenate([away.astype(F32), jnp.zeros((40, PTS), F32)], axis=0).astype(BF16)
    far_ref[:, 208:256] = lax.dot_general(
        chooser, slots, NT, preferred_element_type=F32
    ).astype(BF16)


def pack_kernel(first_rank, cam_ref, pt_ref, res_ref, slot_ref, far_ref, out_ref, feat):
    feat[0:144, 0:PTS] = cam_ref[...]
    feat[144:192, 0:PTS] = pt_ref[...]
    feat[192:208, 0:PTS] = res_ref[...]
    feat[208:224, 0:PTS] = slot_ref[...]
    feat[:, PTS:ALL] = far_ref[...].astype(F32).T[0:ROWS, :].astype(BF16)
    slots = feat[208:224, :].astype(F32)[0:8, :].astype(jnp.int32)
    owner = ((slots + 15) >> 4) - 1
    member = iota((16, ALL), 0)
    touch = jnp.zeros((16, ALL), jnp.bool_)
    for o in range(OBS):
        touch = touch | (jnp.broadcast_to(owner[o : o + 1, :], (16, ALL)) == member)
    hits = touch.astype(F32)
    count = running_count(hits)
    total = jnp.max(count, axis=1, keepdims=True)
    rank = count - 1.0 - first_rank
    rank = jnp.where(touch & (rank >= 0.0) & (rank < CAP), rank, -1.0)
    over = jnp.max((total > CAP).astype(F32), axis=0, keepdims=True)
    seat = iota((CAP, ALL), 0).astype(F32).astype(BF16)
    here = jnp.clip(total - first_rank, 0.0, float(CAP))
    line = iota((16, CAP), 0)
    for d in range(16):
        asked = jnp.broadcast_to(rank[d : d + 1, :], (16, ALL)).astype(BF16)
        asked = jnp.concatenate([asked] * (CAP // 16), axis=0)
        chosen = jnp.where(asked == seat, jnp.asarray(1, BF16), jnp.asarray(0, BF16))
        moved = lax.dot_general(feat[...], chosen, NT, preferred_element_type=F32)
        out_ref[d, 0:208, :] = moved[0:208, :].astype(BF16)
        tail = jnp.where(
            line < 8,
            moved[208:224, :],
            jnp.where(line == 8, here[d : d + 1, :], jnp.where(line == 9, over, 0.0)),
        )
        out_ref[d, 208:224, :] = tail.astype(BF16)


def touched(slots):
    owner = ((slots.astype(jnp.int32) + 15) >> 4) - 1
    member = iota((16, slots.shape[1]), 0)
    touch = jnp.zeros(member.shape, jnp.bool_)
    for o in range(OBS):
        touch = touch | (jnp.broadcast_to(owner[o : o + 1, :], member.shape) == member)
    return touch.astype(F32)


def move(features, rank):
    points = rank.shape[1]
    seat = iota((CAP, points), 0).astype(F32).astype(BF16)
    asked = jnp.broadcast_to(rank, (16, points)).astype(BF16)
    asked = jnp.concatenate([asked] * (CAP // 16), axis=0)
    chosen = jnp.where(asked == seat, jnp.asarray(1, BF16), jnp.asarray(0, BF16))
    return lax.dot_general(features, chosen, NT, preferred_element_type=F32)


def pack_home_kernel(cam_ref, pt_ref, res_ref, slot_ref, out_ref, total_ref, feat):
    feat[0:144, :] = cam_ref[...]
    feat[144:192, :] = pt_ref[...]
    feat[192:208, :] = res_ref[...]
    feat[208:224, :] = slot_ref[...]
    hits = touched(slot_ref[...].astype(F32)[0:8, :])
    count = running_count(hits)
    rank = jnp.where((hits > 0.0) & (count <= CAP), count - 1.0, -1.0)
    total_ref[...] = jnp.broadcast_to(jnp.max(count, axis=1, keepdims=True), (16, 128))
    for d in range(16):
        out_ref[d] = move(feat[...], rank[d : d + 1, :]).astype(BF16)


def pack_arrived_kernel(home_ref, total_ref, far_ref, out_ref, feat, ranks, marks):
    step = pl.program_id(0)

    @pl.when(step == 0)
    def _():
        feat[...] = far_ref[...].astype(F32).T[0:ROWS, :].astype(BF16)
        hits = touched(feat[208:224, :].astype(F32)[0:8, :])
        count = running_count(hits) + total_ref[...]
        total = jnp.max(count, axis=1, keepdims=True)
        ranks[...] = jnp.where((hits > 0.0) & (count <= CAP), count - 1.0, -1.0)
        over = jnp.max((total > CAP).astype(F32), axis=0, keepdims=True)
        marks[0:16, :] = jnp.broadcast_to(jnp.minimum(total, float(CAP)), (16, CAP))
        marks[16:24, :] = jnp.broadcast_to(over, (8, CAP))

    line = iota((16, CAP), 0)
    for i in range(STEP):
        d = step * STEP + i
        moved = move(feat[...], ranks[pl.ds(d, 1), :])
        out_ref[i, 0:208, :] = home_ref[i, 0:208, :] + moved[0:208, :].astype(BF16)
        tail = jnp.where(
            line < 8,
            home_ref[i, 208:224, :].astype(F32) + moved[208:224, :],
            jnp.where(
                line == 8, marks[pl.ds(d, 1), :], jnp.where(line == 9, marks[16:17, :], 0.0)
            ),
        )
        out_ref[i, 208:224, :] = tail.astype(BF16)


def block_values(f):
    slot = f[SLOT : SLOT + 8, :]
    valid = slot > 0.0
    cam = [[f[(k * 9 + a) * 8 : (k * 9 + a) * 8 + 8, :] for a in range(9)] for k in range(2)]
    pt = [
        [
            jnp.where(valid, f[144 + (k * 3 + b) * 8 : 152 + (k * 3 + b) * 8, :], 0.0)
            for b in range(3)
        ]
        for k in range(2)
    ]
    res = [jnp.where(valid, f[192 + k * 8 : 200 + k * 8, :], 0.0) for k in range(2)]

    def over_obs(x):
        return jnp.sum(x, axis=0, keepdims=True)

    v = {}
    for b in range(3):
        for c in range(b, 3):
            v[b, c] = over_obs(pt[0][b] * pt[0][c] + pt[1][b] * pt[1][c]) + (
                DAMPING if b == c else 0.0
            )
            v[c, b] = v[b, c]
    g = [over_obs(pt[0][b] * res[0] + pt[1][b] * res[1]) for b in range(3)]

    def cofactor(i, j):
        r = [x for x in range(3) if x != i]
        c = [x for x in range(3) if x != j]
        minor = v[r[0], c[0]] * v[r[1], c[1]] - v[r[0], c[1]] * v[r[1], c[0]]
        return minor if (i + j) % 2 == 0 else -minor

    cof = {(i, j): cofactor(i, j) for i in range(3) for j in range(i, 3)}
    det = v[0, 0] * cof[0, 0] + v[0, 1] * cof[0, 1] + v[0, 2] * cof[0, 2]
    inv = {}
    for i in range(3):
        for j in range(i, 3):
            inv[i, j] = cof[i, j] / det
            inv[j, i] = inv[i, j]
    w = {}
    z = {}
    for a in range(9):
        for b in range(3):
            w[a, b] = (cam[0][a] * pt[0][b] + cam[1][a] * pt[1][b]).astype(BF16).astype(F32)
        for b in range(3):
            z[a, b] = w[a, 0] * inv[0, b] + w[a, 1] * inv[1, b] + w[a, 2] * inv[2, b]
    return slot, cam, res, w, z, g


def system_kernel(
    blocks, m_ref, x_ref, out_ref, step_ref, wv, iv, wp, zp, ap, gp, tiles, acc, acc_u, acc_g, turned, dm, st, woven, counts
):
    m = m_ref[0]
    acc[...] = jnp.zeros_like(acc)
    acc_u[...] = jnp.zeros_like(acc_u)
    acc_g[...] = jnp.zeros_like(acc_g)
    gp[...] = jnp.zeros_like(gp)
    names = (iota((16, 128), 0) + 1).astype(F32).astype(BF16)

    lane = iota((ROWS, 128), 1)
    place = (iota((16, 128), 0) == COUNT - SLOT) & (iota((16, 128), 1) == 0)
    for s in range(blocks):
        line = x_ref[s, SLOT:ROWS, 0:128].astype(F32)
        counts[s] = jnp.sum(jnp.where(place, line, 0.0)).astype(jnp.int32)

    def append(s, used):
        first = used // 128
        shift = used % 128
        two = [
            pltpu.roll(x_ref[s, :, 0:128].astype(F32), shift, 1),
            pltpu.roll(x_ref[s, :, 128:256].astype(F32), shift, 1),
        ]
        tiles[first] = jnp.where(lane >= shift, two[0], tiles[first])
        tiles[first + 1] = jnp.where(lane < shift, two[0], two[1])
        tiles[first + 2] = jnp.where(lane < shift, two[1], 0.0)
        return used + counts[s]

    tiles[0] = jnp.zeros((ROWS, 128), F32)
    used = lax.fori_loop(0, blocks, append, jnp.int32(0))
    tiles[used // 128 + 1] = jnp.zeros((ROWS, 128), F32)

    def spread(row):
        return jnp.broadcast_to(row, (16, 128)).astype(BF16)

    def seats(slots, own):
        number = jnp.full((16, 128), 8, jnp.int16)
        for o in range(OBS):
            number = jnp.where(slots[o] == own, jnp.int16(o), number)
        return number

    def table(value):
        return jnp.concatenate([value, jnp.zeros_like(value)], axis=0).astype(BF16)

    def seated(values, index):
        return lax.gather(
            values, index[..., None], ALONG_ROWS, (1, 1), mode=lax.GatherScatterMode.PROMISE_IN_BOUNDS
        )

    def chunk(s, carry):
        slot, cam, res, w, z, g = block_values(
            jnp.concatenate([tiles[2 * s], tiles[2 * s + 1]], axis=1)
        )
        for a in range(9):
            for b in range(3):
                wv[(a * 3 + b) * 16 : (a * 3 + b) * 16 + 16, :] = table(w[a, b])
        for b in range(3):
            high = g[b].astype(BF16)
            rest = g[b] - high.astype(F32)
            mid = rest.astype(BF16)
            low = (rest - mid.astype(F32)).astype(BF16)
            rows = jnp.concatenate(
                [high.astype(F32), mid.astype(F32), low.astype(F32), jnp.zeros((13, CAP), F32)], axis=0
            )
            gp[:, b * CAP : (b + 1) * CAP] = rows.astype(BF16)
        mine = ((iota((16, 128), 0) + 1) + m * OWN).astype(F32).astype(BF16)
        for h in range(2):
            lanes = slice(h * 128, h * 128 + 128)
            slots = [spread(slot[o : o + 1, lanes]) for o in range(OBS)]
            for t in range(16):
                iv[t * 16 : t * 16 + 16, lanes] = seats(slots, names + jnp.asarray(16 * t, BF16))
            index = seats(slots, mine)

            def own(value):
                return seated(table(value[:, lanes]), index)

            for a in range(9):
                for b in range(3):
                    zp[a * 16 : a * 16 + 16, b * CAP + h * 128 : b * CAP + h * 128 + 128] = own(
                        z[a, b]
                    )
                for k in range(2):
                    ap[a * 16 : a * 16 + 16, k * CAP + h * 128 : k * CAP + h * 128 + 128] = own(
                        cam[k][a]
                    )
            for k in range(2):
                ap[144:160, k * CAP + h * 128 : k * CAP + h * 128 + 128] = own(res[k])
        acc_u[...] += lax.dot_general(ap[...], ap[0:144, :], NT, preferred_element_type=F32)
        acc_g[...] += lax.dot_general(gp[...], zp[...], NT, preferred_element_type=F32)
        for a in range(9):
            for h in range(2):
                lanes = slice(h * 128, h * 128 + 128)
                values = [wv[(a * 3 + b) * 16 : (a * 3 + b) * 16 + 16, lanes] for b in range(3)]
                for t in range(16):
                    index = iv[t * 16 : t * 16 + 16, lanes]
                    for b in range(3):
                        wp[
                            a * CAMS + t * 16 : a * CAMS + t * 16 + 16,
                            b * CAP + h * 128 : b * CAP + h * 128 + 128,
                        ] = seated(values[b], index)
            if a % 3 == 2:
                three = lax.dot_general(
                    wp[(a - 2) * CAMS : (a + 1) * CAMS, :], zp[...], NT, preferred_element_type=F32
                )
                for q in range(3):
                    acc[a - 2 + q] += three[q * CAMS : (q + 1) * CAMS, :]
        return carry

    lax.fori_loop(0, (used + CAP - 1) // CAP, chunk, 0)

    rows_u = iota((144, 144), 0)
    cols_u = iota((144, 144), 1)
    block = jnp.where((rows_u & 15) == (cols_u & 15), acc_u[0:144, :], 0.0) + jnp.where(
        rows_u == cols_u, DAMPING, 0.0
    )
    grad = jnp.sum(
        jnp.where(iota((16, 144), 0) == (iota((16, 144), 1) & 15), acc_u[144:160, :], 0.0),
        axis=0,
        keepdims=True,
    ) - jnp.sum(acc_g[...], axis=0, keepdims=True)
    dm[...] = jnp.zeros_like(dm)
    own_rows = pl.ds(pl.multiple_of(m * OWN, OWN), OWN)
    for a in range(9):
        acc[a] = -acc[a]
        acc[a, own_rows, :] += block[a * 16 : a * 16 + 16, :]
        dm[a * 16 : a * 16 + 16, 0:144] = acc[a, own_rows, :]
    dm[144:145, 0:144] = grad
    for a in range(9):
        turned[pl.ds(a, CAMS, stride=9), 0:128] = acc[a, :, 0:128]
        st[pl.ds(a, CAMS, stride=9), :] = jnp.concatenate(
            [acc[a, :, 128:144], jnp.zeros((CAMS, 112), F32)], axis=1
        )

    def weave(t):
        lanes = slice(t * 128, t * 128 + 128)
        first = turned[lanes, :].T
        for a in range(8):
            woven[pl.ds(t * 144 + a, 16, stride=9), :] = first[a * 16 : a * 16 + 16, :]
        woven[pl.ds(t * 144 + 8, 16, stride=9), :] = st[lanes, :].T[0:16, :]
        out_ref[:, lanes] = woven[t * 144 : t * 144 + 144, :]

    whole = dm[...]
    flipped = whole.T
    here = iota((8, 256), 1)
    left, right = [], []
    for i in range(18):
        rows = slice(i * 8, i * 8 + 8)
        tile = jnp.where(here < 144, 0.5 * (whole[rows, :] + flipped[rows, :]), flipped[rows, :])
        left.append(tile[:, 0:128])
        right.append(tile[:, 128:256])
    sub = iota((8, 128), 0)
    for k in range(0, 144, PIVOT):
        top = k // 8
        both = k < 128
        cols = []
        for q in range(PIVOT):
            half, c = (left, k + q) if both else (right, k + q - 128)
            cols.append([jnp.broadcast_to(half[i][:, c : c + 1], (8, 128)) for i in range(18)])

        def row_of(tile, q):
            r = (k + q) % 8
            return jnp.broadcast_to(tile[r : r + 1, :], (8, 128))

        piv = [[row_of(cols[j][top], q) for j in range(PIVOT)] for q in range(PIVOT)]
        rhs = [
            ([row_of(left[top], q)] if both else []) + [row_of(right[top], q)] for q in range(PIVOT)
        ]
        for q in range(0, PIVOT, 2):
            a, b, c, d = piv[q][q], piv[q][q + 1], piv[q + 1][q], piv[q + 1][q + 1]
            det = a * d - b * c
            guess = pl.reciprocal(det, approx=True)
            for _ in range(2):
                guess = guess * (2.0 - det * guess)
            ia, ib, ic, id_ = d * guess, b * guess, c * guess, a * guess
            top_two = [piv[q][q + 2 :] + rhs[q], piv[q + 1][q + 2 :] + rhs[q + 1]]
            new = [
                [ia * u - ib * v for u, v in zip(*top_two)],
                [id_ * v - ic * u for u, v in zip(*top_two)],
            ]
            left_over = PIVOT - q - 2
            for r in range(PIVOT):
                if r in (q, q + 1):
                    rest = new[r - q]
                else:
                    rest = [
                        w - piv[r][q] * u - piv[r][q + 1] * v
                        for w, u, v in zip(piv[r][q + 2 :] + rhs[r], *new)
                    ]
                piv[r] = piv[r][: q + 2] + rest[:left_over]
                rhs[r] = rest[left_over:]
        for i in range(18):
            for q in range(PIVOT):
                less = cols[q][i]
                if i == top:
                    less = less - (sub == (k + q) % 8).astype(F32)
                if both:
                    left[i] = left[i] - less * rhs[q][0]
                right[i] = right[i] - less * rhs[q][-1]
        if k % 8 == 0:
            weave(k // 8)
    for i in range(18):
        woven[i * 8 : i * 8 + 8, :] = jnp.broadcast_to(-right[i][:, 16:17], (8, 128))
    for a in range(9):
        st[pl.ds(a, 16, stride=9), :] = woven[a * 16 : a * 16 + 16, :]
    step_ref[...] = st[0:256, :].T[0, 0:144]


def per_device(cam_jac, point_jac, residuals, obs_camera, obs_count, new_cluster, new_slot):
    params = pltpu.CompilerParams(vmem_limit_bytes=VMEM_BYTES)
    vmem = pl.BlockSpec(memory_space=pltpu.VMEM)
    cam = cam_jac.reshape(144, PTS)
    pt = point_jac.reshape(48, PTS)
    res = residuals.reshape(16, PTS)
    slots, far = pl.pallas_call(
        sort_out_kernel,
        out_shape=(jax.ShapeDtypeStruct((16, PTS), BF16), jax.ShapeDtypeStruct((FAR, 256), BF16)),
        in_specs=[vmem] * 7,
        out_specs=(vmem, vmem),
        compiler_params=params,
        name="sort_out",
    )(
        cam,
        pt,
        res,
        obs_camera,
        obs_count.reshape(1, PTS),
        new_cluster.reshape(16, 128),
        new_slot.reshape(16, 128),
    )
    far = lax.all_to_all(
        far.reshape(8, 16, 256), "cluster", split_axis=0, concat_axis=0, tiled=True
    ).reshape(FAR, 256)

    home, home_total = pl.pallas_call(
        pack_home_kernel,
        out_shape=(
            jax.ShapeDtypeStruct((16, ROWS, CAP), BF16),
            jax.ShapeDtypeStruct((16, 128), F32),
        ),
        in_specs=[vmem] * 4,
        out_specs=(vmem, vmem),
        scratch_shapes=[pltpu.VMEM((ROWS, PTS), BF16)],
        compiler_params=params,
        cost_estimate=pl.CostEstimate(flops=2 * 16 * ROWS * PTS * CAP, bytes_accessed=2**21, transcendentals=0),
        name="pack_home",
    )(cam, pt, res, slots)
    first = pl.pallas_call(
        pack_arrived_kernel,
        out_shape=jax.ShapeDtypeStruct((16, ROWS, CAP), BF16),
        grid=(16 // STEP,),
        in_specs=[
            pl.BlockSpec((STEP, ROWS, CAP), lambda g: (g, 0, 0)),
            pl.BlockSpec((16, 128), lambda g: (0, 0)),
            pl.BlockSpec((FAR, 256), lambda g: (0, 0)),
        ],
        out_specs=pl.BlockSpec((STEP, ROWS, CAP), lambda g: (g, 0, 0)),
        scratch_shapes=[
            pltpu.VMEM((ROWS, FAR), BF16),
            pltpu.VMEM((16, 128), F32),
            pltpu.VMEM((24, CAP), F32),
        ],
        compiler_params=params,
        name="pack_arrived",
    )(home, home_total, far)

    def packed(turn):
        def body(*refs):
            pack_kernel(float(turn * CAP), *refs)

        sent = pl.pallas_call(
            body,
            out_shape=jax.ShapeDtypeStruct((16, ROWS, CAP), BF16),
            in_specs=[vmem] * 5,
            out_specs=vmem,
            scratch_shapes=[pltpu.VMEM((ROWS, ALL), BF16)],
            compiler_params=params,
            name="pack",
        )(cam, pt, res, slots, far)
        return lax.all_to_all(sent, "member", split_axis=0, concat_axis=0, tiled=True)

    def system(blocks):
        count = blocks.shape[0]

        def body(*refs):
            system_kernel(count, *refs)

        return pl.pallas_call(
            body,
            out_shape=(
                jax.ShapeDtypeStruct((144, 9 * CAMS), F32),
                jax.ShapeDtypeStruct((144,), F32),
            ),
            in_specs=[pl.BlockSpec(memory_space=pltpu.SMEM), vmem],
            out_specs=(vmem, vmem),
            scratch_shapes=[
                pltpu.VMEM((432, CAP), BF16),
                pltpu.VMEM((CAMS, CAP), jnp.int16),
                pltpu.VMEM((9 * CAMS, 3 * CAP), BF16),
                pltpu.VMEM((144, 3 * CAP), BF16),
                pltpu.VMEM((160, 2 * CAP), BF16),
                pltpu.VMEM((16, 3 * CAP), BF16),
                pltpu.VMEM((2 * count + 2, ROWS, 128), F32),
                pltpu.VMEM((9, CAMS, 144), F32),
                pltpu.VMEM((160, 144), F32),
                pltpu.VMEM((16, 144), F32),
                pltpu.VMEM((9 * CAMS, 128), F32),
                pltpu.VMEM((256, 256), F32),
                pltpu.VMEM((9 * CAMS, 128), F32),
                pltpu.VMEM((18 * 144, 128), F32),
                pltpu.SMEM((count,), jnp.int32),
            ],
            compiler_params=params,
            name="system",
        )(lax.axis_index("member").astype(jnp.int32).reshape(1), blocks)

    arrived = lax.all_to_all(first, "member", split_axis=0, concat_axis=0, tiled=True)

    def more_rounds(arrived):
        return system(jnp.concatenate([arrived] + [packed(t) for t in range(1, ROUNDS)], axis=0))

    matrix, step = lax.cond(jnp.max(arrived[:, OVER, 0]) > 0, more_rounds, system, arrived)
    return matrix, step


def solution(mesh):
    in_specs = (
        P(None, None, ("cluster", "member")),
        P(None, None, ("cluster", "member")),
        P(None, None, ("cluster", "member")),
        P(None, ("cluster", "member")),
        P(("cluster", "member")),
        P(),
        P(),
    )
    out_specs = (P(("cluster", "member"), None), P(("cluster", "member")))
    return jax.shard_map(
        per_device, mesh=mesh, in_specs=in_specs, out_specs=out_specs, check_vma=False
    )
```
